32 devices in a mesh: grp: 2 (over y), ex: 4 (over z), proj: 4 (over x, core).
Axes of the slice: x: 2, y: 2, z: 4, core: 2. Of those that a mesh axis runs over, the one named last changes fastest.
Arguments:
- inputs: bfloat16 [32, 144, 5120], P(('grp', 'ex'), None, 'proj'), parts along dimension 0, may hold values from -6 to 6
- cotangents: bfloat16 [32, 144, 5120], P(('grp', 'ex'), None, 'proj'), parts along dimension 0, may hold values from -6 to 6
- lengths: int32 [32], P(('grp', 'ex')), parts along dimension 0, may hold values from 1 to 144, 1152 in all
- adapter_down_matrix: bfloat16 [128, 5120], P(None, 'proj'), may hold values from -0.078125 to 0.078125
- adapter_up_matrix: bfloat16 [5120, 128], P('proj'), may hold values from -0.078125 to 0.078125
- width_side_sketch: bfloat16 [5120, 512], P('proj'), may hold values from -0.078125 to 0.078125
- rank_side_sketch: bfloat16 [2, 128, 8], replicated, may hold values from -0.5 to 0.5
- heldout_gradient_rows: bfloat16 [256, 8192], P(('grp', 'ex'), 'proj'), parts along dimension 0, may hold values from -20 to 20
Outputs:
- train_proj: bfloat16 [32, 8192], P(('grp', 'ex'), 'proj'), parts along dimension 0
- scores: float32 [32, 128], P(('grp', 'ex'), 'proj'), parts along dimension 0
The draws below stay inside these ranges and needn't reach their ends.
There are 2 independent parts, one for each index of `grp`. The reference program is written for one: setup_inputs(seed, part) draws one part's arguments, and reference() takes and returns one part's arrays. A program takes and returns all parts, laid end to end along the dimension named above; an argument that names none is the same for every part. Nothing has to cross between parts.
Inputs may be any that keep to these rules, and one draw needn't show every extreme that they name: The lengths of each part along grp sum to 1152.
All inputs are finite; a program needn't handle non-finite values. No bound on the sum of `lengths` on one device may be relied on, other than what follows from the above.
Results may differ from the reference program's by a relative error of at most 0.01.
Values may be sent and summed in bfloat16 or wider, within the bound.
No kernel may reach another device: no remote copies, remote signals or barrier semaphores. Data moves between devices by JAX's collectives and lax.ppermute only.
A program may use at most 64 MiB of HBM per device.

```python
import math
import jax
import jax.numpy as jnp
import numpy as np
from jax import lax

MODEL_WIDTH = 5120
ADAPTER_RANK = 128
K1 = 512
K2 = 8
PDIM = 8192
SEQ = 144
EXAMPLES = 16
NVAL = 128


def draw_heldout_gradient_rows(key, part):
    key_base, key_rows, key_cols = jax.random.split(key, 3)
    values = jax.random.normal(key_base, (NVAL, PDIM), jnp.float32)
    values = jnp.clip(values, -4.0, 4.0)
    row_scale = jnp.exp(jax.random.uniform(key_rows, (NVAL, 1), jnp.float32, jnp.log(0.1), 0.0))
    col_scale = jnp.exp(jax.random.uniform(key_cols, (1, PDIM), jnp.float32, jnp.log(0.5), jnp.log(5.0)))
    return (values * row_scale * col_scale).astype(jnp.bfloat16)


def steps_of(rng, dims, pieces, smallest, largest):
    factor_of = 1.0
    for axis_at, parts in pieces:
        heights = jax.random.uniform(jax.random.fold_in(jax.random.fold_in(rng, 6), axis_at), (parts,), jnp.float32, smallest / len(pieces), largest / len(pieces))
        factor_of = factor_of * jnp.repeat(jnp.exp(heights), dims[axis_at] // parts).reshape((-1,) + (1,) * (len(dims) - 1 - axis_at))
    return factor_of


def split_up(number_of, total, most, skew):
    weights = [(1 << 20) // math.isqrt(rank ** skew) + 1 for rank in range(2, number_of + 1)]
    rest, holding = total - most - (number_of - 1), [1] * (number_of - 1)
    while rest > 0:
        candidates = [i for i in range(number_of - 1) if holding[i] < most]
        pool, remaining = sum([weights[i] for i in candidates]), rest
        for i in candidates:
            addition = min(most - holding[i], max(1, remaining * weights[i] // pool), rest)
            holding[i] = holding[i] + addition
            rest = rest - addition
    return np.array([most] + holding)


def uneven(rng, amount, total, bound, lean):
    if amount == 2:
        one = jax.random.randint(rng, (), max(1, total - bound), min(bound, total - 1) + 1)
        return jnp.stack([one, total - one])
    tallies = jnp.asarray(split_up(amount, total, bound, lean), jnp.int32)
    couples = (amount - 1) // 2
    giver, taker = tallies[1:1 + 2 * couples:2], tallies[2:2 + 2 * couples:2]
    room = jnp.minimum(giver - 1, bound - taker)
    passed = jax.random.randint(jax.random.fold_in(rng, 1), (couples,), 0, 1 << 20) % (room + 1)
    tallies = tallies.at[1:1 + 2 * couples:2].set(giver - passed).at[2:2 + 2 * couples:2].set(taker + passed)
    return tallies[jax.random.permutation(jax.random.fold_in(rng, 2), amount)]


def centred(stream_key, extent, width, bound, pieces=(), kind=jnp.bfloat16):
    factor_of = steps_of(stream_key, extent, pieces, -0.22, 0.18) if pieces else 1.0
    array = jax.random.normal(stream_key, extent, jnp.float32) * width * factor_of
    return jnp.minimum(jnp.maximum(array, -bound), bound).astype(kind)


def setup_inputs(seed: int = 0, part: int = 0) -> dict:
    keys = jax.random.split(jax.random.key(seed), 9)
    part_keys = jax.random.split(jax.random.fold_in(keys[8], part), 9)
    return {
        "inputs": centred(part_keys[0], (EXAMPLES, SEQ, MODEL_WIDTH), 1.0, 6.0, ((0, 4), (2, 4))),
        "cotangents": centred(part_keys[1], (EXAMPLES, SEQ, MODEL_WIDTH), 1.0, 6.0, ((0, 4), (2, 4))),
        "lengths": uneven(part_keys[2], EXAMPLES, EXAMPLES * SEQ // 2, SEQ, 2).astype(jnp.int32),
        "adapter_down_matrix": centred(keys[3], (ADAPTER_RANK, MODEL_WIDTH), MODEL_WIDTH ** -0.5, 0.078125, ((1, 4),)),
        "adapter_up_matrix": centred(keys[4], (MODEL_WIDTH, ADAPTER_RANK), MODEL_WIDTH ** -0.5, 0.078125, ((0, 4),)),
        "width_side_sketch": centred(keys[5], (MODEL_WIDTH, K1), MODEL_WIDTH ** -0.5, 0.078125, ((0, 4),)),
        "rank_side_sketch": centred(keys[6], (2, ADAPTER_RANK, K2), ADAPTER_RANK ** -0.5, 0.5),
        "heldout_gradient_rows": draw_heldout_gradient_rows(jax.random.fold_in(jax.random.fold_in(keys[8], part), 71), part),
    }


epsilon = 1e-06

def math_scale():
    return jnp.sqrt(jnp.float32(PDIM))

def reference(inputs, cotangents, lengths, adapter_down_matrix, adapter_up_matrix, width_side_sketch, rank_side_sketch, heldout_gradient_rows):
    row_count = EXAMPLES * SEQ
    flattened_input = inputs.reshape(row_count, MODEL_WIDTH)
    flattened_output = cotangents.reshape(row_count, MODEL_WIDTH)
    rank_side_input = lax.dot_general(flattened_input, adapter_down_matrix, (((1,), (1,)), ((), ())), preferred_element_type=jnp.float32).astype(jnp.bfloat16)
    rank_side_output = jnp.dot(flattened_output, adapter_up_matrix, preferred_element_type=jnp.float32).astype(jnp.bfloat16)
    left_out = jnp.dot(flattened_output, width_side_sketch, preferred_element_type=jnp.float32)
    left_in = jnp.dot(flattened_input, width_side_sketch, preferred_element_type=jnp.float32)
    right_out = jnp.dot(rank_side_input, rank_side_sketch[0], preferred_element_type=jnp.float32).astype(jnp.bfloat16)
    right_in = jnp.dot(rank_side_output, rank_side_sketch[1], preferred_element_type=jnp.float32).astype(jnp.bfloat16)
    left_rows = jnp.stack([left_out, left_in], axis=1).reshape(EXAMPLES, SEQ, 2, K1)
    right_rows = jnp.stack([right_out, right_in], axis=1).reshape(EXAMPLES, SEQ, 2, K2)
    positions = jnp.arange(SEQ, dtype=jnp.int32)
    live_mask = positions[None, :] < lengths[:, None]
    right_rows = jnp.where(live_mask[:, :, None, None], right_rows, jnp.zeros_like(right_rows))
    summed = jnp.einsum('etpk,etpq->ekpq', left_rows.astype(jnp.float32), right_rows.astype(jnp.float32))
    summed = summed / lengths.astype(jnp.float32)[:, None, None, None]
    train_proj = summed.reshape(EXAMPLES, PDIM).astype(jnp.bfloat16)
    train_f32 = train_proj.astype(jnp.float32)
    val_f32 = heldout_gradient_rows.astype(jnp.float32)
    train_sq = lax.optimization_barrier(jnp.sum(train_f32 * train_f32, axis=1))
    val_sq = lax.optimization_barrier(jnp.sum(val_f32 * val_f32, axis=1))
    dot_sums = lax.dot_general(train_proj, heldout_gradient_rows, (((1,), (1,)), ((), ())), preferred_element_type=jnp.float32)
    scores = math_scale() * dot_sums * lax.rsqrt(train_sq + epsilon)[:, None] * lax.rsqrt(val_sq + epsilon)[None, :]
    return (train_proj, scores)
```

```python
import math

import jax
import jax.numpy as jnp
from jax import lax
from jax.sharding import PartitionSpec as P

epsilon = 1e-06


def swap(x, axis, mask):
    size = lax.axis_size(axis)
    return lax.ppermute(x, axis, [(i, i ^ mask) for i in range(size)])


def shards(
    inputs,
    cotangents,
    lengths,
    adapter_down_matrix,
    adapter_up_matrix,
    width_side_sketch,
    rank_side_sketch,
    heldout_gradient_rows,
):
    ex_dev, seq_len, model_cols = inputs.shape
    row_count = ex_dev * seq_len
    k1 = width_side_sketch.shape[1]
    k2 = rank_side_sketch.shape[2]
    n_proj, n_ex = lax.axis_size("proj"), lax.axis_size("ex")
    me_proj, me_ex = lax.axis_index("proj"), lax.axis_index("ex")
    k_own = k1 // n_proj
    pdim = k1 * 2 * k2
    f32, bf16 = jnp.float32, jnp.bfloat16
    acts = inputs.reshape(row_count, model_cols)
    cots = cotangents.reshape(row_count, model_cols)

    if n_ex == n_proj:
        rows = [heldout_gradient_rows] + [swap(heldout_gradient_rows, "ex", m) for m in range(1, n_ex)]
        order = [me_ex ^ m for m in range(n_ex)]
    else:
        every = lax.all_gather(heldout_gradient_rows, "ex", axis=0, tiled=True)
        share = every.shape[0] // n_proj
        rows = [every[s * share : (s + 1) * share] for s in range(n_proj)]
        order = list(range(n_proj))

    down = lax.dot_general(rank_side_sketch[0], adapter_down_matrix, (((0,), (0,)), ((), ())), preferred_element_type=f32)
    up = lax.dot_general(rank_side_sketch[1], adapter_up_matrix, (((0,), (1,)), ((), ())), preferred_element_type=f32)
    right_out = lax.dot_general(down.astype(bf16), acts, (((1,), (1,)), ((), ())), preferred_element_type=f32)
    right_in = lax.dot_general(up.astype(bf16), cots, (((1,), (1,)), ((), ())), preferred_element_type=f32)
    right = jnp.concatenate([right_out, right_in], axis=0)
    right = sum([swap(right, "proj", m) for m in range(1, n_proj)], right).astype(bf16)

    t = jnp.arange(row_count, dtype=jnp.int32)
    e = jnp.arange(ex_dev, dtype=jnp.int32)[:, None]
    live = (t[None, :] >= e * seq_len) & (t[None, :] < e * seq_len + lengths[:, None])
    spread = jnp.where(live[None, :, None, :], right.reshape(2, 1, k2, row_count), jnp.zeros((), bf16))
    spread = spread.reshape(2, ex_dev * k2, row_count)
    parts = []
    for p, rows_of in enumerate((cots, acts)):
        wide = jnp.dot(spread[p], rows_of, preferred_element_type=f32)
        parts.append(jnp.dot(wide.astype(bf16), width_side_sketch, preferred_element_type=f32))
    partial = jnp.concatenate(parts, axis=0)
    own = lax.dynamic_slice_in_dim(partial, me_proj * k_own, k_own, 1)
    for m in range(1, n_proj):
        piece = lax.dynamic_slice_in_dim(partial, (me_proj ^ m) * k_own, k_own, 1)
        own = own + swap(piece, "proj", m)
    own = own.reshape(2, ex_dev, k2, k_own) / lengths.astype(f32)[None, :, None, None]
    train_proj = own.transpose(1, 3, 0, 2).reshape(ex_dev, k_own * 2 * k2).astype(bf16)
    train_f32 = train_proj.astype(f32)
    train_sq = jnp.sum(train_f32 * train_f32, axis=1, keepdims=True)

    notes = []
    for block in rows:
        dots = lax.dot_general(train_proj, block, (((1,), (1,)), ((), ())), preferred_element_type=f32)
        block_f32 = block.astype(f32)
        val_sq = jnp.sum(block_f32 * block_f32, axis=1)[None, :]
        notes.append(jnp.concatenate([dots, val_sq], axis=0))
    notes = jnp.stack(notes)
    train_total = train_sq
    if n_ex == n_proj:
        place = [me_ex ^ me_proj ^ m for m in range(n_proj)]
    else:
        place = [me_proj ^ m for m in range(n_proj)]
    share = notes.shape[2]
    tail = jnp.concatenate([train_sq, jnp.zeros((1, 1), f32)], axis=0)
    total = None
    for m in range(n_proj):
        note = jnp.concatenate([lax.dynamic_index_in_dim(notes, place[m], 0, keepdims=False), tail], axis=1)
        got = note if m == 0 else swap(note, "proj", m)
        total = got if total is None else total + got
    scores = (
        math.sqrt(pdim)
        * total[:ex_dev, :share]
        * lax.rsqrt(total[:ex_dev, share:] + epsilon)
        * lax.rsqrt(total[ex_dev:, :share] + epsilon)
    )
    return (train_proj, scores)


def solution(mesh):
    in_specs = (
        P(("grp", "ex"), None, "proj"),
        P(("grp", "ex"), None, "proj"),
        P(("grp", "ex")),
        P(None, "proj"),
        P("proj", None),
        P("proj", None),
        P(),
        P(("grp", "ex"), "proj"),
    )
    out_specs = (P(("grp", "ex"), "proj"), P(("grp", "ex"), "proj"))
    return jax.shard_map(shards, mesh=mesh, in_specs=in_specs, out_specs=out_specs, check_vma=False)
```

```python
import functools
import math

import jax
import jax.numpy as jnp
from jax import lax
from jax.experimental import pallas as pl
from jax.experimental.pallas import tpu as pltpu
from jax.sharding import PartitionSpec as P

epsilon = 1e-06
LANES = 128
F32, BF16 = jnp.float32, jnp.bfloat16
NT = (((1,), (1,)), ((), ()))
HBM = pl.BlockSpec(memory_space=pl.ANY)
VMEM = pl.BlockSpec(memory_space=pltpu.VMEM)
SMEM = pl.BlockSpec(memory_space=pltpu.SMEM)
PARAMS = pltpu.CompilerParams(vmem_limit_bytes=48 * 1024 * 1024)


def swap(x, axis, mask):
    size = lax.axis_size(axis)
    return lax.ppermute(x, axis, [(i, i ^ mask) for i in range(size)])


def dot(a, b, dims=(((1,), (0,)), ((), ()))):
    return lax.dot_general(a, b, dims, preferred_element_type=F32)


def row_chunks(rows):
    return [(at, min(LANES, rows - at)) for at in range(0, rows, LANES)]


def rank_kernel(acts, cots, down, up, sketch, right, acts_keep, cots_keep, down_v, up_v, sketch_v, sems):
    chunks = row_chunks(acts.shape[0])
    small = [
        pltpu.make_async_copy(src, dst, sems.at[at])
        for at, (src, dst) in enumerate(((sketch, sketch_v), (down, down_v), (up, up_v)))
    ]
    big = []
    for at, rows in chunks:
        for src, dst in ((acts, acts_keep), (cots, cots_keep)):
            cut = pl.ds(at, rows)
            big.append(pltpu.make_async_copy(src.at[cut], dst.at[cut], sems.at[3 + len(big)]))
    for copy in small + big:
        copy.start()
    small[0].wait()
    small[1].wait()
    k2 = sketch.shape[1]
    folded = [dot(sketch_v[0], down_v[...]).astype(BF16)]
    small[2].wait()
    folded.append(dot(sketch_v[1], up_v[...], NT).astype(BF16))
    for at, rows in chunks:
        for p, keep in enumerate((acts_keep, cots_keep)):
            big.pop(0).wait()
            right[p * k2 : (p + 1) * k2, at : at + rows] = dot(folded[p], keep[at : at + rows, :], NT)


def rank_side(acts, cots, down, up, sketch):
    rows, cols = acts.shape
    k2 = sketch.shape[1]
    n_copies = 3 + 2 * len(row_chunks(rows))
    return pl.pallas_call(
        rank_kernel,
        out_shape=(
            jax.ShapeDtypeStruct((2 * k2, rows), F32),
            pltpu.VMEM(acts.shape, BF16),
            pltpu.VMEM(cots.shape, BF16),
        ),
        in_specs=[HBM] * 5,
        out_specs=(VMEM, VMEM, VMEM),
        scratch_shapes=[
            pltpu.VMEM(down.shape, BF16),
            pltpu.VMEM(up.shape, BF16),
            pltpu.VMEM(sketch.shape, BF16),
            pltpu.SemaphoreType.DMA((n_copies,)),
        ],
        compiler_params=PARAMS,
        name="rank_side",
    )(acts, cots, down, up, sketch)


def sums_kernel(n_proj, seq_len, k2, *refs):
    rights, (lengths, acts, cots, width, *outs, parted) = refs[:n_proj], refs[n_proj:]
    right = sum([r[...] for r in rights[1:]], rights[0][...])
    ex_dev, rows = lengths.shape[0], acts.shape[0]
    t = lax.broadcasted_iota(jnp.int32, (k2, rows), 1)
    wide = []
    for p, keep in enumerate((cots, acts)):
        own = right[p * k2 : (p + 1) * k2]
        own = own.astype(BF16).astype(F32)
        spread = [
            jnp.where((t >= e * seq_len) & (t < e * seq_len + lengths[e]), own, 0.0) for e in range(ex_dev)
        ]
        wide.append(dot(jnp.concatenate(spread, axis=0).astype(BF16), keep[...]))
    both = [wide[p][e * k2 : (e + 1) * k2] for e in range(ex_dev) for p in range(2)]
    total = dot(jnp.concatenate(both, axis=0).astype(BF16), width[...])
    k_own = width.shape[1] // n_proj
    for s in range(n_proj):
        parted[s] = total[:, s * k_own : (s + 1) * k_own]
    me = lax.axis_index("proj")
    for m in range(n_proj):
        outs[m][...] = parted[me ^ m]


def token_sums(rights, lengths, acts, cots, width, seq_len, k2):
    n_proj = len(rights)
    ex_dev = lengths.shape[0]
    shape = (ex_dev * 2 * k2, width.shape[1] // n_proj)
    return pl.pallas_call(
        functools.partial(sums_kernel, n_proj, seq_len, k2),
        out_shape=[jax.ShapeDtypeStruct(shape, F32)] * n_proj,
        in_specs=[VMEM] * n_proj + [SMEM] + [VMEM] * 3,
        out_specs=[VMEM] * n_proj,
        scratch_shapes=[pltpu.VMEM((n_proj,) + shape, F32)],
        compiler_params=PARAMS,
        name="token_sums",
    )(*rights, lengths, acts, cots, width)


def dots_kernel(n_proj, r, *refs):
    pieces, lengths, blocks = refs[:n_proj], refs[n_proj], refs[n_proj + 1 : -4]
    train, note, turned, lined = refs[-4:]
    ex_dev = lengths.shape[0]
    k_own = pieces[0].shape[1]
    low = LANES // r
    high = k_own // low
    total = sum([piece[...] for piece in pieces[1:]], pieces[0][...])
    scaled = [total[e * r : (e + 1) * r] / lengths[e].astype(F32) for e in range(ex_dev)]
    turned[:, : ex_dev * r] = jnp.concatenate(scaled, axis=0).T
    lane = lax.broadcasted_iota(jnp.int32, (high, LANES), 1)
    lines = [jnp.zeros((high, LANES), F32)] * ex_dev
    for lo in range(low):
        got = turned[pl.ds(lo, high, stride=low), :]
        for e in range(ex_dev):
            moved = got if lo == e else pltpu.roll(got, (lo - e) * r % LANES, 1)
            lines[e] = jnp.where((lane >= lo * r) & (lane < (lo + 1) * r), moved, lines[e])
    for e in range(ex_dev):
        lined[pl.ds(e, high, stride=ex_dev), :] = lines[e]
    squares = jnp.zeros((ex_dev, LANES), F32)
    for hi in range(high):
        line = lined[hi * ex_dev : (hi + 1) * ex_dev, :].astype(BF16)
        train[:, hi * LANES : (hi + 1) * LANES] = line
        squares += line.astype(F32) * line.astype(F32)
    own = train[...]
    note[...] = jnp.zeros_like(note)
    at, rows, group = 0, 0, []
    for block in blocks:
        for begin in range(0, block.shape[0], LANES):
            size = min(LANES, block.shape[0] - begin)
            group.append(block[begin : begin + size, :])
            rows += size
            if rows == LANES:
                values = jnp.concatenate(group, axis=0)
                note[:ex_dev, at : at + LANES] = dot(own, values, NT)
                square = jnp.zeros((LANES, LANES), F32)
                for c in range(0, values.shape[1], LANES):
                    piece = values[:, c : c + LANES].astype(F32)
                    square += piece * piece
                note[ex_dev : ex_dev + 1, at : at + LANES] = jnp.sum(square.T, axis=0, keepdims=True)
                at, rows, group = at + LANES, 0, []
    note[:ex_dev, at : at + LANES] = jnp.broadcast_to(jnp.sum(squares, axis=1, keepdims=True), (ex_dev, LANES))


def partial_dots(pieces, lengths, blocks, r):
    n_proj, ex_dev = len(pieces), lengths.shape[0]
    k_own = pieces[0].shape[1]
    n_val = sum(block.shape[0] for block in blocks)
    high = k_own * r // LANES
    return pl.pallas_call(
        functools.partial(dots_kernel, n_proj, r),
        out_shape=(
            jax.ShapeDtypeStruct((ex_dev, k_own * r), BF16),
            jax.ShapeDtypeStruct((2 * ex_dev, n_val + LANES), F32),
        ),
        in_specs=[VMEM] * n_proj + [SMEM] + [VMEM] * len(blocks),
        out_specs=(VMEM, VMEM),
        scratch_shapes=[pltpu.VMEM((k_own, LANES), F32), pltpu.VMEM((high * ex_dev, LANES), F32)],
        compiler_params=PARAMS,
        name="partial_dots",
    )(*pieces, lengths, *blocks)


def scores_kernel(n_proj, ex_dev, scale, by_mask, *refs):
    notes, out = refs[:n_proj], refs[n_proj]
    total = sum([note[...] for note in notes[1:]], notes[0][...])
    n_val = total.shape[1] - LANES
    share = out.shape[1]
    train_sq = total[:ex_dev, n_val : n_val + 1]
    val_sq = total[ex_dev : ex_dev + 1, :n_val]
    every = scale * total[:ex_dev, :n_val] * lax.rsqrt(train_sq + epsilon) * lax.rsqrt(val_sq + epsilon)
    at = lax.axis_index("proj")
    if by_mask:
        at = at ^ lax.axis_index("ex")
    whole = jnp.concatenate([every, every], axis=0)
    out[...] = pltpu.roll(whole, (n_val - at * share) % n_val, 1)[:ex_dev, :share]


def final_scores(notes, ex_dev, share, scale, by_mask):
    return pl.pallas_call(
        functools.partial(scores_kernel, len(notes), ex_dev, scale, by_mask),
        out_shape=jax.ShapeDtypeStruct((ex_dev, share), F32),
        in_specs=[VMEM] * len(notes),
        out_specs=VMEM,
        compiler_params=PARAMS,
        name="final_scores",
    )(*notes)


def shards(
    inputs,
    cotangents,
    lengths,
    adapter_down_matrix,
    adapter_up_matrix,
    width_side_sketch,
    rank_side_sketch,
    heldout_gradient_rows,
):
    ex_dev, seq_len, model_cols = inputs.shape
    rows = ex_dev * seq_len
    k1, k2 = width_side_sketch.shape[1], rank_side_sketch.shape[2]
    n_proj, n_ex = lax.axis_size("proj"), lax.axis_size("ex")
    acts = inputs.reshape(rows, model_cols)
    cots = cotangents.reshape(rows, model_cols)

    by_mask = n_ex == n_proj
    if by_mask:
        blocks = [heldout_gradient_rows] + [swap(heldout_gradient_rows, "ex", m) for m in range(1, n_ex)]
    else:
        blocks = [lax.all_gather(heldout_gradient_rows, "ex", axis=0, tiled=True)]

    right, acts, cots = rank_side(
        acts, cots, adapter_down_matrix, adapter_up_matrix, rank_side_sketch.transpose(0, 2, 1)
    )
    rights = [right] + [swap(right, "proj", m) for m in range(1, n_proj)]
    pieces = token_sums(rights, lengths, acts, cots, width_side_sketch, seq_len, k2)
    pieces = [pieces[0]] + [swap(pieces[m], "proj", m) for m in range(1, n_proj)]
    train_proj, note = partial_dots(pieces, lengths, blocks, 2 * k2)
    notes = [note] + [swap(note, "proj", m) for m in range(1, n_proj)]
    share = (note.shape[1] - LANES) // n_proj
    scores = final_scores(notes, ex_dev, share, math.sqrt(k1 * 2 * k2), by_mask)
    return (train_proj, scores)


def solution(mesh):
    in_specs = (
        P(("grp", "ex"), None, "proj"),
        P(("grp", "ex"), None, "proj"),
        P(("grp", "ex")),
        P(None, "proj"),
        P("proj", None),
        P("proj", None),
        P(),
        P(("grp", "ex"), "proj"),
    )
    out_specs = (P(("grp", "ex"), "proj"), P(("grp", "ex"), "proj"))
    return jax.shard_map(shards, mesh=mesh, in_specs=in_specs, out_specs=out_specs, check_vma=False)
```

```python
import functools
import math

import jax
import jax.numpy as jnp
from jax import lax
from jax.experimental import pallas as pl
from jax.experimental.pallas import tpu as pltpu
from jax.sharding import PartitionSpec as P

epsilon = 1e-06
LANES = 128
F32, BF16 = jnp.float32, jnp.bfloat16
NT = (((1,), (1,)), ((), ()))
HBM = pl.BlockSpec(memory_space=pltpu.HBM)
VMEM = pl.BlockSpec(memory_space=pltpu.VMEM)
SMEM = pl.BlockSpec(memory_space=pltpu.SMEM)
PARAMS = pltpu.CompilerParams(vmem_limit_bytes=48 * 1024 * 1024)


def swap(x, axis, mask):
    size = lax.axis_size(axis)
    return lax.ppermute(x, axis, [(i, i ^ mask) for i in range(size)])


def dot(a, b, dims=(((1,), (0,)), ((), ()))):
    return lax.dot_general(a, b, dims, preferred_element_type=F32)


STEP = 2 * LANES


def row_chunks(rows):
    return [(at, min(STEP, rows - at)) for at in range(0, rows, STEP)]


def rank_kernel(acts, cots, down, up, sketch, right, acts_keep, cots_keep, down_v, up_v, sketch_v, sems):
    chunks = row_chunks(acts.shape[0])
    small = [
        pltpu.make_async_copy(src, dst, sems.at[at])
        for at, (src, dst) in enumerate(((sketch, sketch_v), (down, down_v), (up, up_v)))
    ]
    big = []
    for at, rows in chunks:
        for src, dst in ((acts, acts_keep), (cots, cots_keep)):
            cut = pl.ds(at, rows)
            big.append(pltpu.make_async_copy(src.at[cut], dst.at[cut], sems.at[3 + len(big)]))
    for copy in small + big:
        copy.start()
    small[0].wait()
    small[1].wait()
    k2 = sketch.shape[1]
    folded = [dot(sketch_v[0], down_v[...])]
    small[2].wait()
    folded.append(dot(sketch_v[1], up_v[...], NT))
    lanes = acts.shape[1]
    pad = jnp.zeros((LANES - k2, lanes), F32)
    weights = [
        jnp.concatenate([folded[0], pad], axis=0).T.astype(BF16),
        jnp.concatenate([pad[:k2], folded[1], pad[k2:]], axis=0).T.astype(BF16),
    ]
    for at, rows in chunks:
        big.pop(0).wait()
        big.pop(0).wait()
        cut = pl.ds(at, rows)
        got = dot(acts_keep[cut, :], weights[0]) + dot(cots_keep[cut, :], weights[1])
        for b in range(0, rows, LANES):
            size = min(LANES, rows - b)
            right[:, at + b : at + b + size] = got[b : b + size].T[: 2 * k2]


def rank_side(acts, cots, down, up, sketch):
    rows, cols = acts.shape
    k2 = sketch.shape[1]
    n_copies = 3 + 2 * len(row_chunks(rows))
    acts, cots, down, up, sketch = [pltpu.with_memory_space_constraint(x, pltpu.HBM) for x in (acts, cots, down, up, sketch)]
    return pl.pallas_call(
        rank_kernel,
        out_shape=(
            jax.ShapeDtypeStruct((2 * k2, rows), F32),
            pltpu.VMEM(acts.shape, BF16),
            pltpu.VMEM(cots.shape, BF16),
        ),
        in_specs=[HBM] * 5,
        out_specs=(VMEM, VMEM, VMEM),
        scratch_shapes=[
            pltpu.VMEM(down.shape, BF16),
            pltpu.VMEM(up.shape, BF16),
            pltpu.VMEM(sketch.shape, BF16),
            pltpu.SemaphoreType.DMA((n_copies,)),
        ],
        compiler_params=PARAMS,
        name="rank_side",
    )(acts, cots, down, up, sketch)


def sums_kernel(n_proj, seq_len, k2, *refs):
    rights, (lengths, acts, cots, width, *outs, parted) = refs[:n_proj], refs[n_proj:]
    right = sum([r[...] for r in rights[1:]], rights[0][...])
    ex_dev, rows = lengths.shape[0], acts.shape[0]
    t = lax.broadcasted_iota(jnp.int32, (k2, rows), 1)
    wide = []
    for p, keep in enumerate((cots, acts)):
        own = right[p * k2 : (p + 1) * k2]
        own = own.astype(BF16).astype(F32)
        spread = [
            jnp.where((t >= e * seq_len) & (t < e * seq_len + lengths[e]), own, 0.0) for e in range(ex_dev)
        ]
        wide.append(dot(jnp.concatenate(spread, axis=0).astype(BF16), keep[...]))
    both = [wide[p][e * k2 : (e + 1) * k2] for e in range(ex_dev) for p in range(2)]
    total = dot(jnp.concatenate(both, axis=0).astype(BF16), width[...])
    k_own = width.shape[1] // n_proj
    for s in range(n_proj):
        parted[s] = total[:, s * k_own : (s + 1) * k_own]
    me = lax.axis_index("proj")
    for m in range(n_proj):
        outs[m][...] = parted[me ^ m]


def token_sums(rights, lengths, acts, cots, width, seq_len, k2):
    n_proj = len(rights)
    ex_dev = lengths.shape[0]
    shape = (ex_dev * 2 * k2, width.shape[1] // n_proj)
    return pl.pallas_call(
        functools.partial(sums_kernel, n_proj, seq_len, k2),
        out_shape=[jax.ShapeDtypeStruct(shape, F32)] * n_proj,
        in_specs=[VMEM] * n_proj + [SMEM] + [VMEM] * 3,
        out_specs=[VMEM] * n_proj,
        scratch_shapes=[pltpu.VMEM((n_proj,) + shape, F32)],
        compiler_params=PARAMS,
        name="token_sums",
    )(*rights, lengths, acts, cots, width)


def dots_kernel(n_proj, r, *refs):
    pieces, lengths, blocks = refs[:n_proj], refs[n_proj], refs[n_proj + 1 : -4]
    train, note, turned, lined = refs[-4:]
    ex_dev = lengths.shape[0]
    k_own = pieces[0].shape[1]
    low = LANES // r
    high = k_own // low
    total = sum([piece[...] for piece in pieces[1:]], pieces[0][...])
    scaled = [total[e * r : (e + 1) * r] / lengths[e].astype(F32) for e in range(ex_dev)]
    turned[:, : ex_dev * r] = jnp.concatenate(scaled, axis=0).T
    lane = lax.broadcasted_iota(jnp.int32, (high, LANES), 1)
    lines = [jnp.zeros((high, LANES), F32)] * ex_dev
    for lo in range(low):
        got = turned[pl.ds(lo, high, stride=low), :]
        for e in range(ex_dev):
            moved = got if lo == e else pltpu.roll(got, (lo - e) * r % LANES, 1)
            lines[e] = jnp.where((lane >= lo * r) & (lane < (lo + 1) * r), moved, lines[e])
    for e in range(ex_dev):
        lined[pl.ds(e, high, stride=ex_dev), :] = lines[e]
    squares = jnp.zeros((ex_dev, LANES), F32)
    for hi in range(high):
        line = lined[hi * ex_dev : (hi + 1) * ex_dev, :].astype(BF16)
        train[:, hi * LANES : (hi + 1) * LANES] = line
        squares += line.astype(F32) * line.astype(F32)
    own = train[...]
    note[...] = jnp.zeros_like(note)
    at, rows, group = 0, 0, []
    for block in blocks:
        for begin in range(0, block.shape[0], LANES):
            size = min(LANES, block.shape[0] - begin)
            group.append(block[begin : begin + size, :])
            rows += size
            if rows == LANES:
                values = jnp.concatenate(group, axis=0)
                note[:ex_dev, at : at + LANES] = dot(own, values, NT)
                square = jnp.zeros((LANES, LANES), F32)
                for c in range(0, values.shape[1], LANES):
                    piece = values[:, c : c + LANES].astype(F32)
                    square += piece * piece
                note[ex_dev : ex_dev + 1, at : at + LANES] = jnp.sum(square.T, axis=0, keepdims=True)
                at, rows, group = at + LANES, 0, []
    note[:ex_dev, at : at + LANES] = jnp.broadcast_to(jnp.sum(squares, axis=1, keepdims=True), (ex_dev, LANES))


def partial_dots(pieces, lengths, blocks, r):
    n_proj, ex_dev = len(pieces), lengths.shape[0]
    k_own = pieces[0].shape[1]
    n_val = sum(block.shape[0] for block in blocks)
    high = k_own * r // LANES
    return pl.pallas_call(
        functools.partial(dots_kernel, n_proj, r),
        out_shape=(
            jax.ShapeDtypeStruct((ex_dev, k_own * r), BF16),
            jax.ShapeDtypeStruct((2 * ex_dev, n_val + LANES), F32),
        ),
        in_specs=[VMEM] * n_proj + [SMEM] + [VMEM] * len(blocks),
        out_specs=(VMEM, VMEM),
        scratch_shapes=[pltpu.VMEM((k_own, LANES), F32), pltpu.VMEM((high * ex_dev, LANES), F32)],
        compiler_params=PARAMS,
        name="partial_dots",
    )(*pieces, lengths, *blocks)


def scores_kernel(n_proj, ex_dev, scale, by_mask, *refs):
    notes, out = refs[:n_proj], refs[n_proj]
    total = sum([note[...] for note in notes[1:]], notes[0][...])
    n_val = total.shape[1] - LANES
    share = out.shape[1]
    train_sq = total[:ex_dev, n_val : n_val + 1]
    val_sq = total[ex_dev : ex_dev + 1, :n_val]
    every = scale * total[:ex_dev, :n_val] * lax.rsqrt(train_sq + epsilon) * lax.rsqrt(val_sq + epsilon)
    at = lax.axis_index("proj")
    if by_mask:
        at = at ^ lax.axis_index("ex")
    whole = jnp.concatenate([every, every], axis=0)
    out[...] = pltpu.roll(whole, (n_val - at * share) % n_val, 1)[:ex_dev, :share]


def final_scores(notes, ex_dev, share, scale, by_mask):
    return pl.pallas_call(
        functools.partial(scores_kernel, len(notes), ex_dev, scale, by_mask),
        out_shape=jax.ShapeDtypeStruct((ex_dev, share), F32),
        in_specs=[VMEM] * len(notes),
        out_specs=VMEM,
        compiler_params=PARAMS,
        name="final_scores",
    )(*notes)


def shards(
    inputs,
    cotangents,
    lengths,
    adapter_down_matrix,
    adapter_up_matrix,
    width_side_sketch,
    rank_side_sketch,
    heldout_gradient_rows,
):
    ex_dev, seq_len, model_cols = inputs.shape
    rows = ex_dev * seq_len
    k1, k2 = width_side_sketch.shape[1], rank_side_sketch.shape[2]
    n_proj, n_ex = lax.axis_size("proj"), lax.axis_size("ex")
    acts = inputs.reshape(rows, model_cols)
    cots = cotangents.reshape(rows, model_cols)

    by_mask = n_ex == n_proj
    if by_mask:
        blocks = [heldout_gradient_rows] + [swap(heldout_gradient_rows, "ex", m) for m in range(1, n_ex)]
    else:
        blocks = [lax.all_gather(heldout_gradient_rows, "ex", axis=0, tiled=True)]

    right, acts, cots = rank_side(
        acts, cots, adapter_down_matrix, adapter_up_matrix, rank_side_sketch.transpose(0, 2, 1)
    )
    rights = [right] + [swap(right, "proj", m) for m in range(1, n_proj)]
    pieces = token_sums(rights, lengths, acts, cots, width_side_sketch, seq_len, k2)
    pieces = [pieces[0]] + [swap(pieces[m], "proj", m) for m in range(1, n_proj)]
    train_proj, note = partial_dots(pieces, lengths, blocks, 2 * k2)
    notes = [note] + [swap(note, "proj", m) for m in range(1, n_proj)]
    share = (note.shape[1] - LANES) // n_proj
    scores = final_scores(notes, ex_dev, share, math.sqrt(k1 * 2 * k2), by_mask)
    return (train_proj, scores)


def solution(mesh):
    in_specs = (
        P(("grp", "ex"), None, "proj"),
        P(("grp", "ex"), None, "proj"),
        P(("grp", "ex")),
        P(None, "proj"),
        P("proj", None),
        P("proj", None),
        P(),
        P(("grp", "ex"), "proj"),
    )
    out_specs = (P(("grp", "ex"), "proj"), P(("grp", "ex"), "proj"))
    return jax.shard_map(shards, mesh=mesh, in_specs=in_specs, out_specs=out_specs, check_vma=False)
```

```python
import functools
import math

import jax
import jax.numpy as jnp
from jax import lax
from jax.experimental import pallas as pl
from jax.experimental.pallas import tpu as pltpu
from jax.sharding import PartitionSpec as P

epsilon = 1e-06
LANES = 128
F32, BF16 = jnp.float32, jnp.bfloat16
NT = (((1,), (1,)), ((), ()))
HBM = pl.BlockSpec(memory_space=pltpu.HBM)
VMEM = pl.BlockSpec(memory_space=pltpu.VMEM)
SMEM = pl.BlockSpec(memory_space=pltpu.SMEM)
PARAMS = pltpu.CompilerParams(vmem_limit_bytes=48 * 1024 * 1024)


def swap(x, axis, mask):
    size = lax.axis_size(axis)
    return lax.ppermute(x, axis, [(i, i ^ mask) for i in range(size)])


def dot(a, b, dims=(((1,), (0,)), ((), ()))):
    return lax.dot_general(a, b, dims, preferred_element_type=F32)


STEP = 2 * LANES


def row_chunks(rows):
    return [(at, min(STEP, rows - at)) for at in range(0, rows, STEP)]


def rank_kernel(acts, cots, down, up, sketch, right, acts_keep, cots_keep, down_v, up_v, sketch_v, sems):
    chunks = row_chunks(acts.shape[0])
    small = [
        pltpu.make_async_copy(src, dst, sems.at[at])
        for at, (src, dst) in enumerate(((sketch, sketch_v), (down, down_v), (up, up_v)))
    ]
    big = []
    for at, rows in chunks:
        for src, dst in ((acts, acts_keep), (cots, cots_keep)):
            cut = pl.ds(at, rows)
            big.append(pltpu.make_async_copy(src.at[cut], dst.at[cut], sems.at[3 + len(big)]))
    for copy in small + big:
        copy.start()
    small[0].wait()
    small[1].wait()
    k2 = sketch.shape[1]
    folded = [dot(sketch_v[0], down_v[...])]
    small[2].wait()
    folded.append(dot(sketch_v[1], up_v[...], NT))
    lanes = acts.shape[1]
    pad = jnp.zeros((LANES - k2, lanes), F32)
    weights = [
        jnp.concatenate([folded[0], pad], axis=0).T.astype(BF16),
        jnp.concatenate([pad[:k2], folded[1], pad[k2:]], axis=0).T.astype(BF16),
    ]
    for at, rows in chunks:
        big.pop(0).wait()
        big.pop(0).wait()
        cut = pl.ds(at, rows)
        got = dot(acts_keep[cut, :], weights[0]) + dot(cots_keep[cut, :], weights[1])
        for b in range(0, rows, LANES):
            size = min(LANES, rows - b)
            right[:, at + b : at + b + size] = got[b : b + size].T[: 2 * k2]


def rank_side(acts, cots, down, up, sketch):
    rows, cols = acts.shape
    k2 = sketch.shape[1]
    n_copies = 3 + 2 * len(row_chunks(rows))
    acts, cots, down, up, sketch = [pltpu.with_memory_space_constraint(x, pltpu.HBM) for x in (acts, cots, down, up, sketch)]
    return pl.pallas_call(
        rank_kernel,
        out_shape=(
            jax.ShapeDtypeStruct((2 * k2, rows), F32),
            pltpu.VMEM(acts.shape, BF16),
            pltpu.VMEM(cots.shape, BF16),
        ),
        in_specs=[HBM] * 5,
        out_specs=(VMEM, VMEM, VMEM),
        scratch_shapes=[
            pltpu.VMEM(down.shape, BF16),
            pltpu.VMEM(up.shape, BF16),
            pltpu.VMEM(sketch.shape, BF16),
            pltpu.SemaphoreType.DMA((n_copies,)),
        ],
        compiler_params=PARAMS,
        name="rank_side",
    )(acts, cots, down, up, sketch)


def sums_kernel(n_proj, seq_len, k2, *refs):
    rights, (lengths, acts, cots, width, _, *outs, parted) = refs[:n_proj], refs[n_proj:]
    right = sum([r[...] for r in rights[1:]], rights[0][...])
    ex_dev, rows = lengths.shape[0], acts.shape[0]
    t = lax.broadcasted_iota(jnp.int32, (k2, rows), 1)
    wide = []
    for p, keep in enumerate((cots, acts)):
        own = right[p * k2 : (p + 1) * k2]
        own = own.astype(BF16).astype(F32)
        spread = [
            jnp.where((t >= e * seq_len) & (t < e * seq_len + lengths[e]), own, 0.0) for e in range(ex_dev)
        ]
        wide.append(dot(jnp.concatenate(spread, axis=0).astype(BF16), keep[...]))
    both = [wide[p][e * k2 : (e + 1) * k2] for e in range(ex_dev) for p in range(2)]
    total = dot(jnp.concatenate(both, axis=0).astype(BF16), width[...])
    k_own = width.shape[1] // n_proj
    for s in range(n_proj):
        parted[s] = total[:, s * k_own : (s + 1) * k_own]
    me = lax.axis_index("proj")
    for m in range(n_proj):
        outs[m][...] = parted[me ^ m]


def token_sums(rights, lengths, acts, cots, width, seq_len, k2, early):
    n_proj = len(rights)
    ex_dev = lengths.shape[0]
    shape = (ex_dev * 2 * k2, width.shape[1] // n_proj)
    return pl.pallas_call(
        functools.partial(sums_kernel, n_proj, seq_len, k2),
        out_shape=[jax.ShapeDtypeStruct(shape, F32)] * n_proj,
        in_specs=[VMEM] * n_proj + [SMEM] + [VMEM] * 3 + [HBM],
        out_specs=[VMEM] * n_proj,
        scratch_shapes=[pltpu.VMEM((n_proj,) + shape, F32)],
        compiler_params=PARAMS,
        name="token_sums",
        cost_estimate=pl.CostEstimate(flops=20000000000, bytes_accessed=400000000, transcendentals=0),
    )(*rights, lengths, acts, cots, width, early)


def dots_kernel(n_proj, r, *refs):
    pieces, lengths, blocks = refs[:n_proj], refs[n_proj], refs[n_proj + 1 : -4]
    train, note, turned, lined = refs[-4:]
    ex_dev = lengths.shape[0]
    k_own = pieces[0].shape[1]
    low = LANES // r
    high = k_own // low
    total = sum([piece[...] for piece in pieces[1:]], pieces[0][...])
    scaled = [total[e * r : (e + 1) * r] / lengths[e].astype(F32) for e in range(ex_dev)]
    turned[:, : ex_dev * r] = jnp.concatenate(scaled, axis=0).T
    lane = lax.broadcasted_iota(jnp.int32, (high, LANES), 1)
    lines = [jnp.zeros((high, LANES), F32)] * ex_dev
    for lo in range(low):
        got = turned[pl.ds(lo, high, stride=low), :]
        for e in range(ex_dev):
            moved = got if lo == e else pltpu.roll(got, (lo - e) * r % LANES, 1)
            lines[e] = jnp.where((lane >= lo * r) & (lane < (lo + 1) * r), moved, lines[e])
    for e in range(ex_dev):
        lined[pl.ds(e, high, stride=ex_dev), :] = lines[e]
    squares = jnp.zeros((ex_dev, LANES), F32)
    for hi in range(high):
        line = lined[hi * ex_dev : (hi + 1) * ex_dev, :].astype(BF16)
        train[:, hi * LANES : (hi + 1) * LANES] = line
        squares += line.astype(F32) * line.astype(F32)
    own = train[...]
    note[...] = jnp.zeros_like(note)
    at, rows, group = 0, 0, []
    for block in blocks:
        for begin in range(0, block.shape[0], LANES):
            size = min(LANES, block.shape[0] - begin)
            group.append(block[begin : begin + size, :])
            rows += size
            if rows == LANES:
                values = jnp.concatenate(group, axis=0)
                note[:ex_dev, at : at + LANES] = dot(own, values, NT)
                square = jnp.zeros((LANES, LANES), F32)
                for c in range(0, values.shape[1], LANES):
                    piece = values[:, c : c + LANES].astype(F32)
                    square += piece * piece
                note[ex_dev : ex_dev + 1, at : at + LANES] = jnp.sum(square.T, axis=0, keepdims=True)
                at, rows, group = at + LANES, 0, []
    note[:ex_dev, at : at + LANES] = jnp.broadcast_to(jnp.sum(squares, axis=1, keepdims=True), (ex_dev, LANES))


def partial_dots(pieces, lengths, blocks, r):
    n_proj, ex_dev = len(pieces), lengths.shape[0]
    k_own = pieces[0].shape[1]
    n_val = sum(block.shape[0] for block in blocks)
    high = k_own * r // LANES
    return pl.pallas_call(
        functools.partial(dots_kernel, n_proj, r),
        out_shape=(
            pltpu.VMEM((ex_dev, k_own * r), BF16),
            jax.ShapeDtypeStruct((2 * ex_dev, n_val + LANES), F32),
        ),
        in_specs=[VMEM] * n_proj + [SMEM] + [VMEM] * len(blocks),
        out_specs=(VMEM, VMEM),
        scratch_shapes=[pltpu.VMEM((k_own, LANES), F32), pltpu.VMEM((high * ex_dev, LANES), F32)],
        compiler_params=PARAMS,
        name="partial_dots",
    )(*pieces, lengths, *blocks)


def scores_kernel(n_proj, ex_dev, scale, by_mask, *refs):
    notes, out = refs[:n_proj], refs[n_proj]
    total = sum([note[...] for note in notes[1:]], notes[0][...])
    n_val = total.shape[1] - LANES
    share = out.shape[1]
    train_sq = total[:ex_dev, n_val : n_val + 1]
    val_sq = total[ex_dev : ex_dev + 1, :n_val]
    every = scale * total[:ex_dev, :n_val] * lax.rsqrt(train_sq + epsilon) * lax.rsqrt(val_sq + epsilon)
    at = lax.axis_index("proj")
    if by_mask:
        at = at ^ lax.axis_index("ex")
    whole = jnp.concatenate([every, every], axis=0)
    out[...] = pltpu.roll(whole, (n_val - at * share) % n_val, 1)[:ex_dev, :share]


def final_scores(notes, ex_dev, share, scale, by_mask):
    return pl.pallas_call(
        functools.partial(scores_kernel, len(notes), ex_dev, scale, by_mask),
        out_shape=jax.ShapeDtypeStruct((ex_dev, share), F32),
        in_specs=[VMEM] * len(notes),
        out_specs=VMEM,
        compiler_params=PARAMS,
        name="final_scores",
    )(*notes)


def shards(
    inputs,
    cotangents,
    lengths,
    adapter_down_matrix,
    adapter_up_matrix,
    width_side_sketch,
    rank_side_sketch,
    heldout_gradient_rows,
):
    ex_dev, seq_len, model_cols = inputs.shape
    rows = ex_dev * seq_len
    k1, k2 = width_side_sketch.shape[1], rank_side_sketch.shape[2]
    n_proj, n_ex = lax.axis_size("proj"), lax.axis_size("ex")
    acts = inputs.reshape(rows, model_cols)
    cots = cotangents.reshape(rows, model_cols)

    by_mask = n_ex == n_proj
    if by_mask:
        blocks = [heldout_gradient_rows] * n_ex
        blocks[2] = swap(heldout_gradient_rows, "ex", 2)
        blocks[1] = swap(heldout_gradient_rows, "ex", 1)
        blocks[3] = swap(heldout_gradient_rows, "ex", 3)
    else:
        blocks = [lax.all_gather(heldout_gradient_rows, "ex", axis=0, tiled=True)]

    right, acts, cots = rank_side(
        acts, cots, adapter_down_matrix, adapter_up_matrix, rank_side_sketch.transpose(0, 2, 1)
    )
    rights = [right] + [swap(right, "proj", m) for m in range(1, n_proj)]
    pieces = token_sums(rights, lengths, acts, cots, width_side_sketch, seq_len, k2, blocks[min(2, len(blocks) - 1)])
    pieces = [pieces[0]] + [swap(pieces[m], "proj", m) for m in range(1, n_proj)]
    train_proj, note = partial_dots(pieces, lengths, blocks, 2 * k2)
    notes = [note] + [swap(note, "proj", m) for m in range(1, n_proj)]
    share = (note.shape[1] - LANES) // n_proj
    scores = final_scores(notes, ex_dev, share, math.sqrt(k1 * 2 * k2), by_mask)
    return (train_proj, scores)


def solution(mesh):
    in_specs = (
        P(("grp", "ex"), None, "proj"),
        P(("grp", "ex"), None, "proj"),
        P(("grp", "ex")),
        P(None, "proj"),
        P("proj", None),
        P("proj", None),
        P(),
        P(("grp", "ex"), "proj"),
    )
    out_specs = (P(("grp", "ex"), "proj"), P(("grp", "ex"), "proj"))
    return jax.shard_map(shards, mesh=mesh, in_specs=in_specs, out_specs=out_specs, check_vma=False)
```

```python
import functools
import math

import jax
import jax.numpy as jnp
from jax import lax
from jax.experimental import pallas as pl
from jax.experimental.pallas import tpu as pltpu
from jax.sharding import PartitionSpec as P

epsilon = 1e-06
LANES = 128
F32, BF16 = jnp.float32, jnp.bfloat16
NT = (((1,), (1,)), ((), ()))
HBM = pl.BlockSpec(memory_space=pltpu.HBM)
VMEM = pl.BlockSpec(memory_space=pltpu.VMEM)
SMEM = pl.BlockSpec(memory_space=pltpu.SMEM)
PARAMS = pltpu.CompilerParams(vmem_limit_bytes=48 * 1024 * 1024)


def swap(x, axis, mask):
    size = lax.axis_size(axis)
    return lax.ppermute(x, axis, [(i, i ^ mask) for i in range(size)])


def dot(a, b, dims=(((1,), (0,)), ((), ()))):
    return lax.dot_general(a, b, dims, preferred_element_type=F32)


STEP = 2 * LANES


def row_chunks(rows):
    return [(at, min(STEP, rows - at)) for at in range(0, rows, STEP)]


def open_kernel(out):
    out[...] = jnp.zeros_like(out)


def opening():
    return pl.pallas_call(
        open_kernel,
        out_shape=jax.ShapeDtypeStruct((8, LANES), F32),
        out_specs=VMEM,
        compiler_params=PARAMS,
        cost_estimate=pl.CostEstimate(flops=20_000_000_000, bytes_accessed=400_000_000, transcendentals=0),
        name="opening",
    )()


def rank_kernel(acts, cots, down, up, sketch, _, right):
    rows, lanes = acts.shape
    k2 = sketch.shape[1]
    folded = [dot(sketch[0], down[...]), dot(sketch[1], up[...], NT)]
    coarse = [one.astype(BF16).astype(F32) for one in folded]
    fine = [one - near for one, near in zip(folded, coarse)]
    gap = jnp.zeros((k2, lanes), F32)
    pad = jnp.zeros((LANES - 4 * k2, lanes), F32)
    first = jnp.concatenate([coarse[0], gap, fine[0], gap, pad], axis=0).T.astype(BF16)
    second = jnp.concatenate([gap, coarse[1], gap, fine[1], pad], axis=0).T.astype(BF16)
    got = dot(acts[...], first) + dot(cots[...], second)
    for at in range(0, rows, LANES):
        size = min(LANES, rows - at)
        turned = got[at : at + size].T
        right[:, at : at + size] = (turned[: 2 * k2] + turned[2 * k2 : 4 * k2]).astype(right.dtype)


def rank_side(acts, cots, down, up, sketch, gate):
    rows = acts.shape[0]
    return pl.pallas_call(
        rank_kernel,
        out_shape=jax.ShapeDtypeStruct((2 * sketch.shape[1], rows), F32),
        in_specs=[VMEM] * 5 + [HBM],
        out_specs=VMEM,
        compiler_params=PARAMS,
        name="rank_side",
    )(acts, cots, down, up, sketch, gate)


def sums_kernel(n_proj, seq_len, k2, *refs):
    rights, (lengths, acts, cots, width, _, *outs, parted) = refs[:n_proj], refs[n_proj:]
    right = sum([r[...] for r in rights[1:]], rights[0][...])
    ex_dev, rows = lengths.shape[0], acts.shape[0]
    t = lax.broadcasted_iota(jnp.int32, (k2, rows), 1)
    wide = []
    for p, keep in enumerate((cots, acts)):
        own = right[p * k2 : (p + 1) * k2]
        own = own.astype(BF16).astype(F32)
        spread = [
            jnp.where((t >= e * seq_len) & (t < e * seq_len + lengths[e]), own, 0.0) for e in range(ex_dev)
        ]
        wide.append(dot(jnp.concatenate(spread, axis=0).astype(BF16), keep[...]))
    both = [wide[p][e * k2 : (e + 1) * k2] for e in range(ex_dev) for p in range(2)]
    total = dot(jnp.concatenate(both, axis=0).astype(BF16), width[...])
    k_own = width.shape[1] // n_proj
    for s in range(n_proj):
        parted[s] = total[:, s * k_own : (s + 1) * k_own]
    me = lax.axis_index("proj")
    for m in range(n_proj):
        outs[m][...] = parted[me ^ m]


def token_sums(rights, lengths, acts, cots, width, seq_len, k2, early):
    n_proj = len(rights)
    ex_dev = lengths.shape[0]
    shape = (ex_dev * 2 * k2, width.shape[1] // n_proj)
    return pl.pallas_call(
        functools.partial(sums_kernel, n_proj, seq_len, k2),
        out_shape=[jax.ShapeDtypeStruct(shape, F32)] * n_proj,
        in_specs=[VMEM] * n_proj + [SMEM] + [VMEM] * 3 + [HBM],
        out_specs=[VMEM] * n_proj,
        scratch_shapes=[pltpu.VMEM((n_proj,) + shape, F32)],
        compiler_params=PARAMS,
        name="token_sums",
        cost_estimate=pl.CostEstimate(flops=20000000000, bytes_accessed=400000000, transcendentals=0),
    )(*rights, lengths, acts, cots, width, early)


def dots_kernel(n_proj, r, *refs):
    pieces, lengths, blocks = refs[:n_proj], refs[n_proj], refs[n_proj + 1 : -4]
    train, note, turned, lined = refs[-4:]
    ex_dev = lengths.shape[0]
    k_own = pieces[0].shape[1]
    low = LANES // r
    high = k_own // low
    total = sum([piece[...] for piece in pieces[1:]], pieces[0][...])
    scaled = [total[e * r : (e + 1) * r] / lengths[e].astype(F32) for e in range(ex_dev)]
    turned[:, : ex_dev * r] = jnp.concatenate(scaled, axis=0).T
    lane = lax.broadcasted_iota(jnp.int32, (high, LANES), 1)
    lines = [jnp.zeros((high, LANES), F32)] * ex_dev
    for lo in range(low):
        got = turned[pl.ds(lo, high, stride=low), :]
        for e in range(ex_dev):
            moved = got if lo == e else pltpu.roll(got, (lo - e) * r % LANES, 1)
            lines[e] = jnp.where((lane >= lo * r) & (lane < (lo + 1) * r), moved, lines[e])
    for e in range(ex_dev):
        lined[pl.ds(e, high, stride=ex_dev), :] = lines[e]
    squares = jnp.zeros((ex_dev, LANES), F32)
    for hi in range(high):
        line = lined[hi * ex_dev : (hi + 1) * ex_dev, :].astype(BF16)
        train[:, hi * LANES : (hi + 1) * LANES] = line
        squares += line.astype(F32) * line.astype(F32)
    own = train[...]
    note[...] = jnp.zeros_like(note)
    at, rows, group = 0, 0, []
    for block in blocks:
        for begin in range(0, block.shape[0], LANES):
            size = min(LANES, block.shape[0] - begin)
            group.append(block[begin : begin + size, :])
            rows += size
            if rows == LANES:
                values = jnp.concatenate(group, axis=0)
                note[:ex_dev, at : at + LANES] = dot(own, values, NT)
                square = jnp.zeros((LANES, LANES), F32)
                for c in range(0, values.shape[1], LANES):
                    piece = values[:, c : c + LANES].astype(F32)
                    square += piece * piece
                note[ex_dev : ex_dev + 1, at : at + LANES] = jnp.sum(square.T, axis=0, keepdims=True)
                at, rows, group = at + LANES, 0, []
    note[:ex_dev, at : at + LANES] = jnp.broadcast_to(jnp.sum(squares, axis=1, keepdims=True), (ex_dev, LANES))


def partial_dots(pieces, lengths, blocks, r):
    n_proj, ex_dev = len(pieces), lengths.shape[0]
    k_own = pieces[0].shape[1]
    n_val = sum(block.shape[0] for block in blocks)
    high = k_own * r // LANES
    return pl.pallas_call(
        functools.partial(dots_kernel, n_proj, r),
        out_shape=(
            pltpu.VMEM((ex_dev, k_own * r), BF16),
            jax.ShapeDtypeStruct((2 * ex_dev, n_val + LANES), F32),
        ),
        in_specs=[VMEM] * n_proj + [SMEM] + [VMEM] * len(blocks),
        out_specs=(VMEM, VMEM),
        scratch_shapes=[pltpu.VMEM((k_own, LANES), F32), pltpu.VMEM((high * ex_dev, LANES), F32)],
        compiler_params=PARAMS,
        name="partial_dots",
    )(*pieces, lengths, *blocks)


def scores_kernel(n_proj, ex_dev, scale, by_mask, *refs):
    notes, out = refs[:n_proj], refs[n_proj]
    total = sum([note[...] for note in notes[1:]], notes[0][...])
    n_val = total.shape[1] - LANES
    share = out.shape[1]
    train_sq = total[:ex_dev, n_val : n_val + 1]
    val_sq = total[ex_dev : ex_dev + 1, :n_val]
    every = scale * total[:ex_dev, :n_val] * lax.rsqrt(train_sq + epsilon) * lax.rsqrt(val_sq + epsilon)
    at = lax.axis_index("proj")
    if by_mask:
        at = at ^ lax.axis_index("ex")
    whole = jnp.concatenate([every, every], axis=0)
    out[...] = pltpu.roll(whole, (n_val - at * share) % n_val, 1)[:ex_dev, :share]


def final_scores(notes, ex_dev, share, scale, by_mask):
    return pl.pallas_call(
        functools.partial(scores_kernel, len(notes), ex_dev, scale, by_mask),
        out_shape=jax.ShapeDtypeStruct((ex_dev, share), F32),
        in_specs=[VMEM] * len(notes),
        out_specs=VMEM,
        compiler_params=PARAMS,
        name="final_scores",
    )(*notes)


def shards(
    inputs,
    cotangents,
    lengths,
    adapter_down_matrix,
    adapter_up_matrix,
    width_side_sketch,
    rank_side_sketch,
    heldout_gradient_rows,
):
    ex_dev, seq_len, model_cols = inputs.shape
    rows = ex_dev * seq_len
    k1, k2 = width_side_sketch.shape[1], rank_side_sketch.shape[2]
    n_proj, n_ex = lax.axis_size("proj"), lax.axis_size("ex")
    acts = inputs.reshape(rows, model_cols)
    cots = cotangents.reshape(rows, model_cols)

    by_mask = n_ex == n_proj
    if by_mask:
        gate, held = lax.optimization_barrier((opening(), heldout_gradient_rows))
        blocks = [heldout_gradient_rows] * n_ex
        blocks[2] = swap(held, "ex", 2)
    else:
        gate = opening()
        blocks = [lax.all_gather(heldout_gradient_rows, "ex", axis=0, tiled=True)]

    right = rank_side(
        acts, cots, adapter_down_matrix, adapter_up_matrix, rank_side_sketch.transpose(0, 2, 1), gate
    )
    rights = [right] + [swap(right, "proj", m) for m in range(1, n_proj)]
    if by_mask:
        later, rights[1] = lax.optimization_barrier((heldout_gradient_rows, rights[1]))
        blocks[3] = swap(later, "ex", 3)
        blocks[1] = swap(later, "ex", 1)
    pieces = token_sums(rights, lengths, acts, cots, width_side_sketch, seq_len, k2, blocks[min(2, len(blocks) - 1)])
    pieces = [pieces[0]] + [swap(pieces[m], "proj", m) for m in range(1, n_proj)]
    train_proj, note = partial_dots(pieces, lengths, blocks, 2 * k2)
    notes = [note] + [swap(note, "proj", m) for m in range(1, n_proj)]
    share = (note.shape[1] - LANES) // n_proj
    scores = final_scores(notes, ex_dev, share, math.sqrt(k1 * 2 * k2), by_mask)
    return (train_proj, scores)


def solution(mesh):
    in_specs = (
        P(("grp", "ex"), None, "proj"),
        P(("grp", "ex"), None, "proj"),
        P(("grp", "ex")),
        P(None, "proj"),
        P("proj", None),
        P("proj", None),
        P(),
        P(("grp", "ex"), "proj"),
    )
    out_specs = (P(("grp", "ex"), "proj"), P(("grp", "ex"), "proj"))
    return jax.shard_map(shards, mesh=mesh, in_specs=in_specs, out_specs=out_specs, check_vma=False)
```

```python
import functools
import math

import jax
import jax.numpy as jnp
from jax import lax
from jax.experimental import pallas as pl
from jax.experimental.pallas import tpu as pltpu
from jax.sharding import PartitionSpec as P

epsilon = 1e-06
LANES = 128
F32, BF16 = jnp.float32, jnp.bfloat16
NT = (((1,), (1,)), ((), ()))
HBM = pl.BlockSpec(memory_space=pltpu.HBM)
VMEM = pl.BlockSpec(memory_space=pltpu.VMEM)
SMEM = pl.BlockSpec(memory_space=pltpu.SMEM)
PARAMS = pltpu.CompilerParams(vmem_limit_bytes=48 * 1024 * 1024)


def swap(x, axis, mask):
    size = lax.axis_size(axis)
    return lax.ppermute(x, axis, [(i, i ^ mask) for i in range(size)])


def dot(a, b, dims=(((1,), (0,)), ((), ()))):
    return lax.dot_general(a, b, dims, preferred_element_type=F32)


STEP = 2 * LANES


def row_chunks(rows):
    return [(at, min(STEP, rows - at)) for at in range(0, rows, STEP)]


def open_kernel(out):
    out[...] = jnp.zeros_like(out)


def opening():
    return pl.pallas_call(
        open_kernel,
        out_shape=pltpu.VMEM((8, LANES), F32),
        out_specs=VMEM,
        compiler_params=pltpu.CompilerParams(vmem_limit_bytes=63400000),
        cost_estimate=pl.CostEstimate(flops=20_000_000_000, bytes_accessed=400_000_000, transcendentals=0),
        name="opening",
    )()


def rank_kernel(acts, cots, down, up, sketch, _, right):
    rows, lanes = acts.shape
    k2 = sketch.shape[1]
    folded = [dot(sketch[0], down[...]), dot(sketch[1], up[...], NT)]
    coarse = [one.astype(BF16).astype(F32) for one in folded]
    fine = [one - near for one, near in zip(folded, coarse)]
    gap = jnp.zeros((k2, lanes), F32)
    pad = jnp.zeros((LANES - 4 * k2, lanes), F32)
    first = jnp.concatenate([coarse[0], gap, fine[0], gap, pad], axis=0).T.astype(BF16)
    second = jnp.concatenate([gap, coarse[1], gap, fine[1], pad], axis=0).T.astype(BF16)
    got = dot(acts[...], first) + dot(cots[...], second)
    for at in range(0, rows, LANES):
        size = min(LANES, rows - at)
        turned = got[at : at + size].T
        right[:, at : at + size] = (turned[: 2 * k2] + turned[2 * k2 : 4 * k2]).astype(right.dtype)


def rank_side(acts, cots, down, up, sketch, gate):
    rows = acts.shape[0]
    return pl.pallas_call(
        rank_kernel,
        out_shape=jax.ShapeDtypeStruct((2 * sketch.shape[1], rows), F32),
        in_specs=[VMEM] * 5 + [pl.BlockSpec(memory_space=pl.ANY)],
        out_specs=VMEM,
        compiler_params=PARAMS,
        name="rank_side",
    )(acts, cots, down, up, sketch, gate)


def sums_kernel(n_proj, seq_len, k2, *refs):
    rights, (lengths, acts, cots, width, *outs, parted) = refs[:n_proj], refs[n_proj:]
    right = sum([r[...] for r in rights[1:]], rights[0][...])
    ex_dev, rows = lengths.shape[1], acts.shape[0]
    t = lax.broadcasted_iota(jnp.int32, (k2, rows), 1)
    wide = []
    for p, keep in enumerate((cots, acts)):
        own = right[p * k2 : (p + 1) * k2]
        own = own.astype(BF16).astype(F32)
        spread = [
            jnp.where((t >= e * seq_len) & (t < e * seq_len + lengths[:, e : e + 1]), own, 0.0) for e in range(ex_dev)
        ]
        wide.append(dot(jnp.concatenate(spread, axis=0).astype(BF16), keep[...]))
    both = [wide[p][e * k2 : (e + 1) * k2] for e in range(ex_dev) for p in range(2)]
    total = dot(jnp.concatenate(both, axis=0).astype(BF16), width[...])
    k_own = width.shape[1] // n_proj
    for s in range(n_proj):
        parted[s] = total[:, s * k_own : (s + 1) * k_own]
    me = lax.axis_index("proj")
    for m in range(n_proj):
        outs[m][...] = parted[me ^ m].astype(BF16)


def token_sums(rights, lengths, acts, cots, width, seq_len, k2):
    n_proj = len(rights)
    ex_dev = lengths.shape[1]
    shape = (ex_dev * 2 * k2, width.shape[1] // n_proj)
    return pl.pallas_call(
        functools.partial(sums_kernel, n_proj, seq_len, k2),
        out_shape=[jax.ShapeDtypeStruct(shape, BF16)] * n_proj,
        in_specs=[VMEM] * n_proj + [VMEM] + [VMEM] * 3,
        out_specs=[VMEM] * n_proj,
        scratch_shapes=[pltpu.VMEM((n_proj,) + shape, F32)],
        compiler_params=PARAMS,
        name="token_sums",
        cost_estimate=pl.CostEstimate(flops=20000000000, bytes_accessed=400000000, transcendentals=0),
    )(*rights, lengths, acts, cots, width)


def dots_kernel(n_proj, r, *refs):
    pieces, lengths, blocks = refs[:n_proj], refs[n_proj], refs[n_proj + 1 : -4]
    train, note, turned, lined = refs[-4:]
    ex_dev = lengths.shape[1]
    k_own = pieces[0].shape[1]
    low = LANES // r
    high = k_own // low
    total = sum([piece[...].astype(F32) for piece in pieces[1:]], pieces[0][...].astype(F32))
    scaled = [total[e * r : (e + 1) * r] / lengths[:, e : e + 1].astype(F32) for e in range(ex_dev)]
    turned[:, : ex_dev * r] = jnp.concatenate(scaled, axis=0).T
    lane = lax.broadcasted_iota(jnp.int32, (high, LANES), 1)
    lines = [jnp.zeros((high, LANES), F32)] * ex_dev
    for lo in range(low):
        got = turned[pl.ds(lo, high, stride=low), :]
        for e in range(ex_dev):
            moved = got if lo == e else pltpu.roll(got, (lo - e) * r % LANES, 1)
            lines[e] = jnp.where((lane >= lo * r) & (lane < (lo + 1) * r), moved, lines[e])
    for e in range(ex_dev):
        lined[pl.ds(e, high, stride=ex_dev), :] = lines[e]
    squares = jnp.zeros((ex_dev, LANES), F32)
    for hi in range(high):
        line = lined[hi * ex_dev : (hi + 1) * ex_dev, :].astype(BF16)
        train[:, hi * LANES : (hi + 1) * LANES] = line
        squares += line.astype(F32) * line.astype(F32)
    own = train[...]
    note[...] = jnp.zeros_like(note)
    at, rows, group = 0, 0, []
    for block in blocks:
        for begin in range(0, block.shape[0], LANES):
            size = min(LANES, block.shape[0] - begin)
            group.append(block[begin : begin + size, :])
            rows += size
            if rows == LANES:
                values = jnp.concatenate(group, axis=0)
                note[:ex_dev, at : at + LANES] = dot(own, values, NT)
                square = jnp.zeros((LANES, LANES), F32)
                for c in range(0, values.shape[1], LANES):
                    piece = values[:, c : c + LANES].astype(F32)
                    square += piece * piece
                note[ex_dev : ex_dev + 1, at : at + LANES] = jnp.sum(square.T, axis=0, keepdims=True)
                at, rows, group = at + LANES, 0, []
    note[:ex_dev, at : at + LANES] = jnp.broadcast_to(jnp.sum(squares, axis=1, keepdims=True), (ex_dev, LANES))


def partial_dots(pieces, lengths, blocks, r):
    n_proj, ex_dev = len(pieces), lengths.shape[1]
    k_own = pieces[0].shape[1]
    n_val = sum(block.shape[0] for block in blocks)
    high = k_own * r // LANES
    return pl.pallas_call(
        functools.partial(dots_kernel, n_proj, r),
        out_shape=(
            pltpu.VMEM((ex_dev, k_own * r), BF16),
            jax.ShapeDtypeStruct((2 * ex_dev, n_val + LANES), F32),
        ),
        in_specs=[VMEM] * n_proj + [VMEM] + [VMEM] * len(blocks),
        out_specs=(VMEM, VMEM),
        scratch_shapes=[pltpu.VMEM((k_own, LANES), F32), pltpu.VMEM((high * ex_dev, LANES), F32)],
        compiler_params=PARAMS,
        name="partial_dots",
    )(*pieces, lengths, *blocks)


def scores_kernel(n_proj, ex_dev, scale, by_mask, *refs):
    notes, out = refs[:n_proj], refs[n_proj]
    total = sum([note[...] for note in notes[1:]], notes[0][...])
    n_val = total.shape[1] - LANES
    share = out.shape[1]
    train_sq = total[:ex_dev, n_val : n_val + 1]
    val_sq = total[ex_dev : ex_dev + 1, :n_val]
    every = scale * total[:ex_dev, :n_val] * lax.rsqrt(train_sq + epsilon) * lax.rsqrt(val_sq + epsilon)
    at = lax.axis_index("proj")
    if by_mask:
        at = at ^ lax.axis_index("ex")
    whole = jnp.concatenate([every, every], axis=0)
    out[...] = pltpu.roll(whole, (n_val - at * share) % n_val, 1)[:ex_dev, :share]


def final_scores(notes, ex_dev, share, scale, by_mask):
    return pl.pallas_call(
        functools.partial(scores_kernel, len(notes), ex_dev, scale, by_mask),
        out_shape=jax.ShapeDtypeStruct((ex_dev, share), F32),
        in_specs=[VMEM] * len(notes),
        out_specs=VMEM,
        compiler_params=PARAMS,
        name="final_scores",
    )(*notes)


def shards(
    inputs,
    cotangents,
    lengths,
    adapter_down_matrix,
    adapter_up_matrix,
    width_side_sketch,
    rank_side_sketch,
    heldout_gradient_rows,
):
    ex_dev, seq_len, model_cols = inputs.shape
    rows = ex_dev * seq_len
    k1, k2 = width_side_sketch.shape[1], rank_side_sketch.shape[2]
    n_proj, n_ex = lax.axis_size("proj"), lax.axis_size("ex")
    lengths = lengths.reshape(1, ex_dev)
    acts = inputs.reshape(rows, model_cols)
    cots = cotangents.reshape(rows, model_cols)

    by_mask = n_ex == n_proj
    if by_mask:
        gate, held = lax.optimization_barrier((opening(), heldout_gradient_rows))
        blocks = [heldout_gradient_rows] * n_ex
        blocks[2] = swap(held, "ex", 2)
    else:
        gate = opening()
        blocks = [lax.all_gather(heldout_gradient_rows, "ex", axis=0, tiled=True)]

    right = rank_side(
        acts, cots, adapter_down_matrix, adapter_up_matrix, rank_side_sketch.transpose(0, 2, 1), gate
    )
    rights = [right] + [swap(right, "proj", m) for m in range(1, n_proj)]
    if by_mask:
        blocks[1] = swap(heldout_gradient_rows, "ex", 1)
        blocks[3] = swap(blocks[2], "ex", 1)
    pieces = token_sums(rights, lengths, acts, cots, width_side_sketch, seq_len, k2)
    pieces = [pieces[0]] + [swap(pieces[m], "proj", m) for m in range(1, n_proj)]
    train_proj, note = partial_dots(pieces, lengths, blocks, 2 * k2)
    notes = [note] + [swap(note, "proj", m) for m in range(1, n_proj)]
    share = (note.shape[1] - LANES) // n_proj
    scores = final_scores(notes, ex_dev, share, math.sqrt(k1 * 2 * k2), by_mask)
    return (train_proj, scores)


def solution(mesh):
    in_specs = (
        P(("grp", "ex"), None, "proj"),
        P(("grp", "ex"), None, "proj"),
        P(("grp", "ex")),
        P(None, "proj"),
        P("proj", None),
        P("proj", None),
        P(),
        P(("grp", "ex"), "proj"),
    )
    out_specs = (P(("grp", "ex"), "proj"), P(("grp", "ex"), "proj"))
    return jax.shard_map(shards, mesh=mesh, in_specs=in_specs, out_specs=out_specs, check_vma=False)
```

```python
import functools
import math

import jax
import jax.numpy as jnp
from jax import lax
from jax.experimental import pallas as pl
from jax.experimental.pallas import tpu as pltpu
from jax.sharding import PartitionSpec as P

epsilon = 1e-06
LANES = 128
PLANES = 4
F32, BF16 = jnp.float32, jnp.bfloat16
NT = (((1,), (1,)), ((), ()))
HBM = pl.BlockSpec(memory_space=pltpu.HBM)
VMEM = pl.BlockSpec(memory_space=pltpu.VMEM)
PARAMS = pltpu.CompilerParams(vmem_limit_bytes=48 * 1024 * 1024)


def swap(x, axis, mask):
    size = lax.axis_size(axis)
    return lax.ppermute(x, axis, [(i, i ^ mask) for i in range(size)])


def dot(a, b, dims=(((1,), (0,)), ((), ()))):
    return lax.dot_general(a, b, dims, preferred_element_type=F32)


def open_kernel(out):
    out[...] = jnp.zeros_like(out)


def opening():
    return pl.pallas_call(
        open_kernel,
        out_shape=pltpu.VMEM((8, LANES), F32),
        out_specs=VMEM,
        compiler_params=pltpu.CompilerParams(vmem_limit_bytes=63400000),
        cost_estimate=pl.CostEstimate(flops=20_000_000_000, bytes_accessed=400_000_000, transcendentals=0),
        name="opening",
    )()


def rank_kernel(acts, cots, down, up, sketch, _, right):
    rows, lanes = acts.shape
    k2 = sketch.shape[1]
    folded = [dot(sketch[0], down[...]), dot(sketch[1], up[...], NT)]
    coarse = [one.astype(BF16).astype(F32) for one in folded]
    fine = [one - near for one, near in zip(folded, coarse)]
    gap = jnp.zeros((k2, lanes), F32)
    pad = jnp.zeros((LANES - 4 * k2, lanes), F32)
    first = jnp.concatenate([coarse[0], gap, fine[0], gap, pad], axis=0).T.astype(BF16)
    second = jnp.concatenate([gap, coarse[1], gap, fine[1], pad], axis=0).T.astype(BF16)
    got = dot(acts[...], first) + dot(cots[...], second)
    for at in range(0, rows, LANES):
        size = min(LANES, rows - at)
        turned = got[at : at + size].T
        right[:, at : at + size] = (turned[: 2 * k2] + turned[2 * k2 : 4 * k2]).astype(right.dtype)


def rank_side(acts, cots, down, up, sketch, gate):
    rows = acts.shape[0]
    return pl.pallas_call(
        rank_kernel,
        out_shape=jax.ShapeDtypeStruct((2 * sketch.shape[1], rows), F32),
        in_specs=[VMEM] * 5 + [pl.BlockSpec(memory_space=pl.ANY)],
        out_specs=VMEM,
        compiler_params=PARAMS,
        name="rank_side",
    )(acts, cots, down, up, sketch, gate)


def sums_kernel(n_proj, seq_len, k2, *refs):
    rights, (lengths, acts, cots, width, *outs, parted) = refs[:n_proj], refs[n_proj:]
    right = sum([r[...] for r in rights[1:]], rights[0][...])
    ex_dev, rows = lengths.shape[1], acts.shape[0]
    t = lax.broadcasted_iota(jnp.int32, (k2, rows), 1)
    wide = []
    for p, keep in enumerate((cots, acts)):
        own = right[p * k2 : (p + 1) * k2]
        own = own.astype(BF16).astype(F32)
        spread = [
            jnp.where((t >= e * seq_len) & (t < e * seq_len + lengths[:, e : e + 1]), own, 0.0) for e in range(ex_dev)
        ]
        wide.append(dot(jnp.concatenate(spread, axis=0).astype(BF16), keep[...]))
    both = [wide[p][e * k2 : (e + 1) * k2] for e in range(ex_dev) for p in range(2)]
    total = dot(jnp.concatenate(both, axis=0).astype(BF16), width[...])
    k_own = width.shape[1] // n_proj
    for s in range(n_proj):
        parted[s] = total[:, s * k_own : (s + 1) * k_own]
    me = lax.axis_index("proj")
    for m in range(n_proj):
        outs[m][...] = parted[me ^ m].astype(outs[m].dtype)


def token_sums(rights, lengths, acts, cots, width, seq_len, k2):
    n_proj = len(rights)
    ex_dev = lengths.shape[1]
    shape = (ex_dev * 2 * k2, width.shape[1] // n_proj)
    return pl.pallas_call(
        functools.partial(sums_kernel, n_proj, seq_len, k2),
        out_shape=[jax.ShapeDtypeStruct(shape, F32)] + [jax.ShapeDtypeStruct(shape, BF16)] * (n_proj - 1),
        in_specs=[VMEM] * n_proj + [VMEM] + [VMEM] * 3,
        out_specs=[VMEM] * n_proj,
        scratch_shapes=[pltpu.VMEM((n_proj,) + shape, F32)],
        compiler_params=PARAMS,
        name="token_sums",
        cost_estimate=pl.CostEstimate(flops=20000000000, bytes_accessed=400000000, transcendentals=0),
    )(*rights, lengths, acts, cots, width)


def dots_kernel(n_proj, r, *refs):
    pieces, lengths, blocks = refs[:n_proj], refs[n_proj], refs[n_proj + 1 : -4]
    train, note, turned, lined = refs[-4:]
    ex_dev = lengths.shape[1]
    k_own = pieces[0].shape[1]
    low = LANES // r
    high = k_own // low
    total = sum([piece[...].astype(F32) for piece in pieces[1:]], pieces[0][...].astype(F32))
    scaled = [total[e * r : (e + 1) * r] / lengths[:, e : e + 1].astype(F32) for e in range(ex_dev)]
    turned[:, : ex_dev * r] = jnp.concatenate(scaled, axis=0).T
    lane = lax.broadcasted_iota(jnp.int32, (high, LANES), 1)
    lines = [jnp.zeros((high, LANES), F32)] * ex_dev
    for lo in range(low):
        got = turned[pl.ds(lo, high, stride=low), :]
        for e in range(ex_dev):
            moved = got if lo == e else pltpu.roll(got, (lo - e) * r % LANES, 1)
            lines[e] = jnp.where((lane >= lo * r) & (lane < (lo + 1) * r), moved, lines[e])
    for e in range(ex_dev):
        lined[pl.ds(e, high, stride=ex_dev), :] = lines[e]
    squares = jnp.zeros((ex_dev, LANES), F32)
    for hi in range(high):
        line = lined[hi * ex_dev : (hi + 1) * ex_dev, :].astype(BF16)
        train[:, hi * LANES : (hi + 1) * LANES] = line
        squares += line.astype(F32) * line.astype(F32)
    own = train[...]
    note[...] = jnp.zeros_like(note)
    at, rows, group = 0, 0, []
    for block in blocks:
        for begin in range(0, block.shape[0], LANES):
            size = min(LANES, block.shape[0] - begin)
            group.append(block[begin : begin + size, :])
            rows += size
            if rows == LANES:
                values = jnp.concatenate(group, axis=0)
                note[:ex_dev, at : at + LANES] = dot(own, values, NT)
                square = jnp.zeros((LANES, LANES), F32)
                for c in range(0, values.shape[1], LANES):
                    piece = values[:, c : c + LANES].astype(F32)
                    square += piece * piece
                note[ex_dev : ex_dev + 1, at : at + LANES] = jnp.sum(square.T, axis=0, keepdims=True)
                at, rows, group = at + LANES, 0, []
    note[:ex_dev, at : at + LANES] = jnp.broadcast_to(jnp.sum(squares, axis=1, keepdims=True), (ex_dev, LANES))


def partial_dots(pieces, lengths, blocks, r):
    n_proj, ex_dev = len(pieces), lengths.shape[1]
    k_own = pieces[0].shape[1]
    n_val = sum(block.shape[0] for block in blocks)
    high = k_own * r // LANES
    return pl.pallas_call(
        functools.partial(dots_kernel, n_proj, r),
        out_shape=(
            pltpu.VMEM((ex_dev, k_own * r), BF16),
            jax.ShapeDtypeStruct((2 * ex_dev, n_val + LANES), F32),
        ),
        in_specs=[VMEM] * n_proj + [VMEM] + [VMEM] * len(blocks),
        out_specs=(VMEM, VMEM),
        scratch_shapes=[pltpu.VMEM((k_own, LANES), F32), pltpu.VMEM((high * ex_dev, LANES), F32)],
        compiler_params=PARAMS,
        name="partial_dots",
    )(*pieces, lengths, *blocks)


def scores_kernel(n_proj, ex_dev, scale, by_mask, *refs):
    notes, out = refs[:n_proj], refs[n_proj]
    total = sum([note[...] for note in notes[1:]], notes[0][...])
    n_val = total.shape[1] - LANES
    share = out.shape[1]
    train_sq = total[:ex_dev, n_val : n_val + 1]
    val_sq = total[ex_dev : ex_dev + 1, :n_val]
    every = scale * total[:ex_dev, :n_val] * lax.rsqrt(train_sq + epsilon) * lax.rsqrt(val_sq + epsilon)
    at = lax.axis_index("proj")
    if by_mask:
        at = at ^ lax.axis_index("ex")
    whole = jnp.concatenate([every, every], axis=0)
    out[...] = pltpu.roll(whole, (n_val - at * share) % n_val, 1)[:ex_dev, :share]


def final_scores(notes, ex_dev, share, scale, by_mask):
    return pl.pallas_call(
        functools.partial(scores_kernel, len(notes), ex_dev, scale, by_mask),
        out_shape=jax.ShapeDtypeStruct((ex_dev, share), F32),
        in_specs=[VMEM] * len(notes),
        out_specs=VMEM,
        compiler_params=PARAMS,
        name="final_scores",
    )(*notes)


def shards(
    inputs,
    cotangents,
    lengths,
    adapter_down_matrix,
    adapter_up_matrix,
    width_side_sketch,
    rank_side_sketch,
    heldout_gradient_rows,
):
    ex_dev, seq_len, model_cols = inputs.shape
    rows = ex_dev * seq_len
    k1, k2 = width_side_sketch.shape[1], rank_side_sketch.shape[2]
    n_proj, n_ex = lax.axis_size("proj"), lax.axis_size("ex")
    lengths = lengths.reshape(1, ex_dev)
    acts = inputs.reshape(rows, model_cols)
    cots = cotangents.reshape(rows, model_cols)

    by_mask = n_ex == n_proj == PLANES
    if by_mask:
        gate, held = lax.optimization_barrier((opening(), heldout_gradient_rows))
        blocks = [heldout_gradient_rows] * n_ex
        blocks[2] = swap(held, "ex", 2)
    else:
        gate = opening()
        blocks = [lax.all_gather(heldout_gradient_rows, "ex", axis=0, tiled=True)]

    right = rank_side(
        acts, cots, adapter_down_matrix, adapter_up_matrix, rank_side_sketch.transpose(0, 2, 1), gate
    )
    rights = [right] + [swap(right, "proj", m) for m in range(n_proj - 1, 0, -1)]
    if by_mask:
        blocks[1] = swap(heldout_gradient_rows, "ex", 1)
        blocks[3] = swap(blocks[2], "ex", 1)
    pieces = token_sums(rights, lengths, acts, cots, width_side_sketch, seq_len, k2)
    pieces = [pieces[0]] + [swap(pieces[m], "proj", m) for m in range(n_proj - 1, 0, -1)]
    train_proj, note = partial_dots(pieces, lengths, blocks, 2 * k2)
    notes = [note] + [swap(note, "proj", m) for m in range(n_proj - 1, 0, -1)]
    share = (note.shape[1] - LANES) // n_proj
    scores = final_scores(notes, ex_dev, share, math.sqrt(k1 * 2 * k2), by_mask)
    return (train_proj, scores)


def solution(mesh):
    in_specs = (
        P(("grp", "ex"), None, "proj"),
        P(("grp", "ex"), None, "proj"),
        P(("grp", "ex")),
        P(None, "proj"),
        P("proj", None),
        P("proj", None),
        P(),
        P(("grp", "ex"), "proj"),
    )
    out_specs = (P(("grp", "ex"), "proj"), P(("grp", "ex"), "proj"))
    return jax.shard_map(shards, mesh=mesh, in_specs=in_specs, out_specs=out_specs, check_vma=False)
```

```python
import functools
import math

import jax
import jax.numpy as jnp
from jax import lax
from jax.experimental import pallas as pl
from jax.experimental.pallas import tpu as pltpu
from jax.sharding import PartitionSpec as P

epsilon = 1e-06
LANES = 128
PLANES = 4
F32, BF16 = jnp.float32, jnp.bfloat16
NT = (((1,), (1,)), ((), ()))
HBM = pl.BlockSpec(memory_space=pltpu.HBM)
VMEM = pl.BlockSpec(memory_space=pltpu.VMEM)
PARAMS = pltpu.CompilerParams(vmem_limit_bytes=48 * 1024 * 1024)


def swap(x, axis, mask):
    size = lax.axis_size(axis)
    return lax.ppermute(x, axis, [(i, i ^ mask) for i in range(size)])


def dot(a, b, dims=(((1,), (0,)), ((), ()))):
    return lax.dot_general(a, b, dims, preferred_element_type=F32)


def open_kernel(out):
    out[...] = jnp.zeros_like(out)


def opening():
    return pl.pallas_call(
        open_kernel,
        out_shape=pltpu.VMEM((8, LANES), F32),
        out_specs=VMEM,
        compiler_params=pltpu.CompilerParams(vmem_limit_bytes=63400000),
        cost_estimate=pl.CostEstimate(flops=20_000_000_000, bytes_accessed=400_000_000, transcendentals=0),
        name="opening",
    )()


def rank_kernel(acts, cots, down, up, sketch, _, right):
    rows, lanes = acts.shape
    k2 = sketch.shape[1]
    folded = [dot(sketch[0], down[...]), dot(sketch[1], up[...], NT)]
    coarse = [one.astype(BF16).astype(F32) for one in folded]
    fine = [one - near for one, near in zip(folded, coarse)]
    gap = jnp.zeros((k2, lanes), F32)
    pad = jnp.zeros((LANES - 4 * k2, lanes), F32)
    first = jnp.concatenate([coarse[0], gap, fine[0], gap, pad], axis=0).T.astype(BF16)
    second = jnp.concatenate([gap, coarse[1], gap, fine[1], pad], axis=0).T.astype(BF16)
    got = dot(acts[...], first) + dot(cots[...], second)
    for at in range(0, rows, LANES):
        size = min(LANES, rows - at)
        turned = got[at : at + size].T
        right[:, at : at + size] = (turned[: 2 * k2] + turned[2 * k2 : 4 * k2]).astype(right.dtype)


def rank_side(acts, cots, down, up, sketch, gate):
    rows = acts.shape[0]
    return pl.pallas_call(
        rank_kernel,
        out_shape=jax.ShapeDtypeStruct((2 * sketch.shape[1], rows), F32),
        in_specs=[VMEM] * 5 + [pl.BlockSpec(memory_space=pl.ANY)],
        out_specs=VMEM,
        compiler_params=PARAMS,
        name="rank_side",
    )(acts, cots, down, up, sketch, gate)


def sums_kernel(n_proj, seq_len, k2, *refs):
    rights, (lengths, acts, cots, width, *outs, parted) = refs[:n_proj], refs[n_proj:]
    right = sum([r[...] for r in rights[1:]], rights[0][...])
    ex_dev, rows = lengths.shape[1], acts.shape[0]
    t = lax.broadcasted_iota(jnp.int32, (k2, rows), 1)
    wide = []
    for p, keep in enumerate((cots, acts)):
        own = right[p * k2 : (p + 1) * k2]
        own = own.astype(BF16).astype(F32)
        spread = [
            jnp.where((t >= e * seq_len) & (t < e * seq_len + lengths[:, e : e + 1]), own, 0.0) for e in range(ex_dev)
        ]
        wide.append(dot(jnp.concatenate(spread, axis=0).astype(BF16), keep[...]))
    both = [wide[p][e * k2 : (e + 1) * k2] for e in range(ex_dev) for p in range(2)]
    total = dot(jnp.concatenate(both, axis=0).astype(BF16), width[...])
    k_own = width.shape[1] // n_proj
    for s in range(n_proj):
        parted[s] = total[:, s * k_own : (s + 1) * k_own]
    me = lax.axis_index("proj")
    for m in range(n_proj):
        outs[m][...] = parted[me ^ m].astype(outs[m].dtype)


def token_sums(rights, lengths, acts, cots, width, seq_len, k2):
    n_proj = len(rights)
    ex_dev = lengths.shape[1]
    shape = (ex_dev * 2 * k2, width.shape[1] // n_proj)
    return pl.pallas_call(
        functools.partial(sums_kernel, n_proj, seq_len, k2),
        out_shape=[jax.ShapeDtypeStruct(shape, F32)] + [jax.ShapeDtypeStruct(shape, BF16)] * (n_proj - 1),
        in_specs=[VMEM] * n_proj + [VMEM] + [VMEM] * 3,
        out_specs=[VMEM] * n_proj,
        scratch_shapes=[pltpu.VMEM((n_proj,) + shape, F32)],
        compiler_params=PARAMS,
        name="token_sums",
        cost_estimate=pl.CostEstimate(flops=20000000000, bytes_accessed=400000000, transcendentals=0),
    )(*rights, lengths, acts, cots, width)


def dots_kernel(n_proj, r, *refs):
    pieces, lengths, blocks = refs[:n_proj], refs[n_proj], refs[n_proj + 1 : -4]
    train, note, turned, lined = refs[-4:]
    ex_dev = lengths.shape[1]
    k_own = pieces[0].shape[1]
    low = LANES // r
    high = k_own // low
    total = sum([piece[...].astype(F32) for piece in pieces[1:]], pieces[0][...].astype(F32))
    scaled = [total[e * r : (e + 1) * r] / lengths[:, e : e + 1].astype(F32) for e in range(ex_dev)]
    turned[:, : ex_dev * r] = jnp.concatenate(scaled, axis=0).T
    lane = lax.broadcasted_iota(jnp.int32, (high, LANES), 1)
    lines = [jnp.zeros((high, LANES), F32)] * ex_dev
    for lo in range(low):
        got = turned[pl.ds(lo, high, stride=low), :]
        for e in range(ex_dev):
            moved = got if lo == e else pltpu.roll(got, (lo - e) * r % LANES, 1)
            lines[e] = jnp.where((lane >= lo * r) & (lane < (lo + 1) * r), moved, lines[e])
    for e in range(ex_dev):
        lined[pl.ds(e, high, stride=ex_dev), :] = lines[e]
    squares = jnp.zeros((ex_dev, LANES), F32)
    for hi in range(high):
        line = lined[hi * ex_dev : (hi + 1) * ex_dev, :].astype(BF16)
        train[:, hi * LANES : (hi + 1) * LANES] = line
        squares += line.astype(F32) * line.astype(F32)
    own = train[...]
    note[...] = jnp.zeros_like(note)
    at, rows, group = 0, 0, []
    for block in blocks:
        for begin in range(0, block.shape[0], LANES):
            size = min(LANES, block.shape[0] - begin)
            group.append(block[begin : begin + size, :])
            rows += size
            if rows == LANES:
                values = jnp.concatenate(group, axis=0)
                note[:ex_dev, at : at + LANES] = dot(own, values, NT)
                square = jnp.zeros((LANES, LANES), F32)
                for c in range(0, values.shape[1], LANES):
                    piece = values[:, c : c + LANES].astype(F32)
                    square += piece * piece
                note[ex_dev : ex_dev + 1, at : at + LANES] = jnp.sum(square.T, axis=0, keepdims=True)
                at, rows, group = at + LANES, 0, []
    note[:ex_dev, at : at + LANES] = jnp.broadcast_to(jnp.sum(squares, axis=1, keepdims=True), (ex_dev, LANES))


def partial_dots(pieces, lengths, blocks, r):
    n_proj, ex_dev = len(pieces), lengths.shape[1]
    k_own = pieces[0].shape[1]
    n_val = sum(block.shape[0] for block in blocks)
    high = k_own * r // LANES
    return pl.pallas_call(
        functools.partial(dots_kernel, n_proj, r),
        out_shape=(
            pltpu.VMEM((ex_dev, k_own * r), BF16),
            jax.ShapeDtypeStruct((2 * ex_dev, n_val + LANES), F32),
        ),
        in_specs=[VMEM] * n_proj + [VMEM] + [VMEM] * len(blocks),
        out_specs=(VMEM, VMEM),
        scratch_shapes=[pltpu.VMEM((k_own, LANES), F32), pltpu.VMEM((high * ex_dev, LANES), F32)],
        compiler_params=PARAMS,
        name="partial_dots",
    )(*pieces, lengths, *blocks)


def scores_kernel(n_proj, ex_dev, scale, by_mask, *refs):
    notes, out = refs[:n_proj], refs[n_proj]
    total = sum([note[...] for note in notes[1:]], notes[0][...])
    n_val = total.shape[1] - LANES
    share = out.shape[1]
    train_sq = total[:ex_dev, n_val : n_val + 1]
    val_sq = total[ex_dev : ex_dev + 1, :n_val]
    every = scale * total[:ex_dev, :n_val] * lax.rsqrt(train_sq + epsilon) * lax.rsqrt(val_sq + epsilon)
    at = lax.axis_index("proj")
    if by_mask:
        at = at ^ lax.axis_index("ex")
    whole = jnp.concatenate([every, every], axis=0)
    out[...] = pltpu.roll(whole, (n_val - at * share) % n_val, 1)[:ex_dev, :share]


def final_scores(notes, ex_dev, share, scale, by_mask):
    return pl.pallas_call(
        functools.partial(scores_kernel, len(notes), ex_dev, scale, by_mask),
        out_shape=jax.ShapeDtypeStruct((ex_dev, share), F32),
        in_specs=[VMEM] * len(notes),
        out_specs=VMEM,
        compiler_params=PARAMS,
        name="final_scores",
    )(*notes)


def shards(
    inputs,
    cotangents,
    lengths,
    adapter_down_matrix,
    adapter_up_matrix,
    width_side_sketch,
    rank_side_sketch,
    heldout_gradient_rows,
):
    ex_dev, seq_len, model_cols = inputs.shape
    rows = ex_dev * seq_len
    k1, k2 = width_side_sketch.shape[1], rank_side_sketch.shape[2]
    n_proj, n_ex = lax.axis_size("proj"), lax.axis_size("ex")
    lengths = lengths.reshape(1, ex_dev)
    acts = inputs.reshape(rows, model_cols)
    cots = cotangents.reshape(rows, model_cols)

    by_mask = n_ex == n_proj == PLANES
    if by_mask:
        gate, held = lax.optimization_barrier((opening(), heldout_gradient_rows))
        blocks = [heldout_gradient_rows] * n_ex
        blocks[2] = swap(held, "ex", 2)
    else:
        gate = opening()
        blocks = [lax.all_gather(heldout_gradient_rows, "ex", axis=0, tiled=True)]

    right = rank_side(
        acts, cots, adapter_down_matrix, adapter_up_matrix, rank_side_sketch.transpose(0, 2, 1), gate
    )
    rights = [right] + [swap(right, "proj", m) for m in range(1, n_proj)]
    if by_mask:
        blocks[1] = swap(heldout_gradient_rows, "ex", 1)
        blocks[3] = swap(blocks[2], "ex", 1)
    pieces = token_sums(rights, lengths, acts, cots, width_side_sketch, seq_len, k2)
    pieces = [pieces[0]] + [swap(pieces[m], "proj", m) for m in range(n_proj - 1, 0, -1)]
    train_proj, note = partial_dots(pieces, lengths, blocks, 2 * k2)
    notes = [note] + [swap(note, "proj", m) for m in range(1, n_proj)]
    share = (note.shape[1] - LANES) // n_proj
    scores = final_scores(notes, ex_dev, share, math.sqrt(k1 * 2 * k2), by_mask)
    return (train_proj, scores)


def solution(mesh):
    in_specs = (
        P(("grp", "ex"), None, "proj"),
        P(("grp", "ex"), None, "proj"),
        P(("grp", "ex")),
        P(None, "proj"),
        P("proj", None),
        P("proj", None),
        P(),
        P(("grp", "ex"), "proj"),
    )
    out_specs = (P(("grp", "ex"), "proj"), P(("grp", "ex"), "proj"))
    return jax.shard_map(shards, mesh=mesh, in_specs=in_specs, out_specs=out_specs, check_vma=False)
```

```python
import functools
import math

import jax
import jax.numpy as jnp
from jax import lax
from jax.experimental import pallas as pl
from jax.experimental.pallas import tpu as pltpu
from jax.sharding import PartitionSpec as P

epsilon = 1e-06
LANES = 128
PLANES = 4
F32, BF16 = jnp.float32, jnp.bfloat16
NT = (((1,), (1,)), ((), ()))
HBM = pl.BlockSpec(memory_space=pltpu.HBM)
VMEM = pl.BlockSpec(memory_space=pltpu.VMEM)
PARAMS = pltpu.CompilerParams(vmem_limit_bytes=48 * 1024 * 1024)


def swap(x, axis, mask):
    size = lax.axis_size(axis)
    return lax.ppermute(x, axis, [(i, i ^ mask) for i in range(size)])


def dot(a, b, dims=(((1,), (0,)), ((), ()))):
    return lax.dot_general(a, b, dims, preferred_element_type=F32)


def open_kernel(out):
    out[...] = jnp.zeros_like(out)


def opening():
    return pl.pallas_call(
        open_kernel,
        out_shape=pltpu.VMEM((8, LANES), F32),
        out_specs=VMEM,
        compiler_params=pltpu.CompilerParams(vmem_limit_bytes=63400000),
        cost_estimate=pl.CostEstimate(flops=20_000_000_000, bytes_accessed=400_000_000, transcendentals=0),
        name="opening",
    )()


def rank_kernel(acts, cots, down, up, sketch, _, right):
    rows, lanes = acts.shape
    k2 = sketch.shape[1]
    folded = [dot(sketch[0], down[...]), dot(sketch[1], up[...], NT)]
    coarse = [one.astype(BF16).astype(F32) for one in folded]
    fine = [one - near for one, near in zip(folded, coarse)]
    gap = jnp.zeros((k2, lanes), F32)
    pad = jnp.zeros((LANES - 4 * k2, lanes), F32)
    first = jnp.concatenate([coarse[0], gap, fine[0], gap, pad], axis=0).T.astype(BF16)
    second = jnp.concatenate([gap, coarse[1], gap, fine[1], pad], axis=0).T.astype(BF16)
    got = dot(acts[...], first) + dot(cots[...], second)
    for at in range(0, rows, LANES):
        size = min(LANES, rows - at)
        turned = got[at : at + size].T
        right[:, at : at + size] = (turned[: 2 * k2] + turned[2 * k2 : 4 * k2]).astype(right.dtype)


def rank_side(acts, cots, down, up, sketch, gate):
    rows = acts.shape[0]
    return pl.pallas_call(
        rank_kernel,
        out_shape=jax.ShapeDtypeStruct((2 * sketch.shape[1], rows), BF16),
        in_specs=[VMEM] * 5 + [pl.BlockSpec(memory_space=pl.ANY)],
        out_specs=VMEM,
        compiler_params=PARAMS,
        name="rank_side",
    )(acts, cots, down, up, sketch, gate)


def sums_kernel(n_proj, seq_len, k2, *refs):
    rights, (lengths, acts, cots, width, *outs, parted) = refs[:n_proj], refs[n_proj:]
    right = sum([r[...].astype(F32) for r in rights[1:]], rights[0][...].astype(F32))
    ex_dev, rows = lengths.shape[1], acts.shape[0]
    t = lax.broadcasted_iota(jnp.int32, (k2, rows), 1)
    wide = []
    for p, keep in enumerate((cots, acts)):
        own = right[p * k2 : (p + 1) * k2]
        own = own.astype(BF16).astype(F32)
        spread = [
            jnp.where((t >= e * seq_len) & (t < e * seq_len + lengths[:, e : e + 1]), own, 0.0) for e in range(ex_dev)
        ]
        wide.append(dot(jnp.concatenate(spread, axis=0).astype(BF16), keep[...]))
    both = [wide[p][e * k2 : (e + 1) * k2] for e in range(ex_dev) for p in range(2)]
    total = dot(jnp.concatenate(both, axis=0).astype(BF16), width[...])
    k_own = width.shape[1] // n_proj
    for s in range(n_proj):
        parted[s] = total[:, s * k_own : (s + 1) * k_own]
    me = lax.axis_index("proj")
    for m in range(n_proj):
        outs[m][...] = parted[me ^ m].astype(outs[m].dtype)


def token_sums(rights, lengths, acts, cots, width, seq_len, k2):
    n_proj = len(rights)
    ex_dev = lengths.shape[1]
    shape = (ex_dev * 2 * k2, width.shape[1] // n_proj)
    return pl.pallas_call(
        functools.partial(sums_kernel, n_proj, seq_len, k2),
        out_shape=[jax.ShapeDtypeStruct(shape, F32)] + [jax.ShapeDtypeStruct(shape, BF16)] * (n_proj - 1),
        in_specs=[VMEM] * n_proj + [VMEM] + [VMEM] * 3,
        out_specs=[VMEM] * n_proj,
        scratch_shapes=[pltpu.VMEM((n_proj,) + shape, F32)],
        compiler_params=PARAMS,
        name="token_sums",
        cost_estimate=pl.CostEstimate(flops=20000000000, bytes_accessed=400000000, transcendentals=0),
    )(*rights, lengths, acts, cots, width)


def dots_kernel(n_proj, r, *refs):
    pieces, lengths, blocks = refs[:n_proj], refs[n_proj], refs[n_proj + 1 : -4]
    train, note, turned, lined = refs[-4:]
    ex_dev = lengths.shape[1]
    k_own = pieces[0].shape[1]
    low = LANES // r
    high = k_own // low
    total = sum([piece[...].astype(F32) for piece in pieces[1:]], pieces[0][...].astype(F32))
    scaled = [total[e * r : (e + 1) * r] / lengths[:, e : e + 1].astype(F32) for e in range(ex_dev)]
    turned[:, : ex_dev * r] = jnp.concatenate(scaled, axis=0).T
    lane = lax.broadcasted_iota(jnp.int32, (high, LANES), 1)
    lines = [jnp.zeros((high, LANES), F32)] * ex_dev
    for lo in range(low):
        got = turned[pl.ds(lo, high, stride=low), :]
        for e in range(ex_dev):
            moved = got if lo == e else pltpu.roll(got, (lo - e) * r % LANES, 1)
            lines[e] = jnp.where((lane >= lo * r) & (lane < (lo + 1) * r), moved, lines[e])
    for e in range(ex_dev):
        lined[pl.ds(e, high, stride=ex_dev), :] = lines[e]
    squares = jnp.zeros((ex_dev, LANES), F32)
    for hi in range(high):
        line = lined[hi * ex_dev : (hi + 1) * ex_dev, :].astype(BF16)
        train[:, hi * LANES : (hi + 1) * LANES] = line
        squares += line.astype(F32) * line.astype(F32)
    own = train[...]
    note[...] = jnp.zeros_like(note)
    at, rows, group = 0, 0, []
    for block in blocks:
        for begin in range(0, block.shape[0], LANES):
            size = min(LANES, block.shape[0] - begin)
            group.append(block[begin : begin + size, :])
            rows += size
            if rows == LANES:
                values = jnp.concatenate(group, axis=0)
                note[:ex_dev, at : at + LANES] = dot(own, values, NT)
                square = jnp.zeros((LANES, LANES), F32)
                for c in range(0, values.shape[1], LANES):
                    piece = values[:, c : c + LANES].astype(F32)
                    square += piece * piece
                note[ex_dev : ex_dev + 1, at : at + LANES] = jnp.sum(square.T, axis=0, keepdims=True)
                at, rows, group = at + LANES, 0, []
    note[:ex_dev, at : at + LANES] = jnp.broadcast_to(jnp.sum(squares, axis=1, keepdims=True), (ex_dev, LANES))


def partial_dots(pieces, lengths, blocks, r):
    n_proj, ex_dev = len(pieces), lengths.shape[1]
    k_own = pieces[0].shape[1]
    n_val = sum(block.shape[0] for block in blocks)
    high = k_own * r // LANES
    return pl.pallas_call(
        functools.partial(dots_kernel, n_proj, r),
        out_shape=(
            pltpu.VMEM((ex_dev, k_own * r), BF16),
            jax.ShapeDtypeStruct((2 * ex_dev, n_val + LANES), F32),
        ),
        in_specs=[VMEM] * n_proj + [VMEM] + [VMEM] * len(blocks),
        out_specs=(VMEM, VMEM),
        scratch_shapes=[pltpu.VMEM((k_own, LANES), F32), pltpu.VMEM((high * ex_dev, LANES), F32)],
        compiler_params=PARAMS,
        name="partial_dots",
    )(*pieces, lengths, *blocks)


def scores_kernel(n_proj, ex_dev, scale, by_mask, *refs):
    notes, out = refs[:n_proj], refs[n_proj]
    total = sum([note[...] for note in notes[1:]], notes[0][...])
    n_val = total.shape[1] - LANES
    share = out.shape[1]
    train_sq = total[:ex_dev, n_val : n_val + 1]
    val_sq = total[ex_dev : ex_dev + 1, :n_val]
    every = scale * total[:ex_dev, :n_val] * lax.rsqrt(train_sq + epsilon) * lax.rsqrt(val_sq + epsilon)
    at = lax.axis_index("proj")
    if by_mask:
        at = at ^ lax.axis_index("ex")
    whole = jnp.concatenate([every, every], axis=0)
    out[...] = pltpu.roll(whole, (n_val - at * share) % n_val, 1)[:ex_dev, :share]


def final_scores(notes, ex_dev, share, scale, by_mask):
    return pl.pallas_call(
        functools.partial(scores_kernel, len(notes), ex_dev, scale, by_mask),
        out_shape=jax.ShapeDtypeStruct((ex_dev, share), F32),
        in_specs=[VMEM] * len(notes),
        out_specs=VMEM,
        compiler_params=PARAMS,
        name="final_scores",
    )(*notes)


def shards(
    inputs,
    cotangents,
    lengths,
    adapter_down_matrix,
    adapter_up_matrix,
    width_side_sketch,
    rank_side_sketch,
    heldout_gradient_rows,
):
    ex_dev, seq_len, model_cols = inputs.shape
    rows = ex_dev * seq_len
    k1, k2 = width_side_sketch.shape[1], rank_side_sketch.shape[2]
    n_proj, n_ex = lax.axis_size("proj"), lax.axis_size("ex")
    lengths = lengths.reshape(1, ex_dev)
    acts = inputs.reshape(rows, model_cols)
    cots = cotangents.reshape(rows, model_cols)

    by_mask = n_ex == n_proj == PLANES
    if by_mask:
        gate, held = lax.optimization_barrier((opening(), heldout_gradient_rows))
        blocks = [heldout_gradient_rows] * n_ex
        blocks[3] = swap(held, "ex", 3)
    else:
        gate = opening()
        blocks = [lax.all_gather(heldout_gradient_rows, "ex", axis=0, tiled=True)]

    right = rank_side(
        acts, cots, adapter_down_matrix, adapter_up_matrix, rank_side_sketch.transpose(0, 2, 1), gate
    )
    rights = [right] + [swap(right, "proj", m) for m in range(1, n_proj)]
    if by_mask:
        blocks[1] = swap(heldout_gradient_rows, "ex", 1)
        blocks[2] = swap(blocks[3], "ex", 1)
    pieces = token_sums(rights, lengths, acts, cots, width_side_sketch, seq_len, k2)
    pieces = [pieces[0]] + [swap(pieces[m], "proj", m) for m in range(n_proj - 1, 0, -1)]
    train_proj, note = partial_dots(pieces, lengths, blocks, 2 * k2)
    notes = [note] + [swap(note, "proj", m) for m in range(1, n_proj)]
    share = (note.shape[1] - LANES) // n_proj
    scores = final_scores(notes, ex_dev, share, math.sqrt(k1 * 2 * k2), by_mask)
    return (train_proj, scores)


def solution(mesh):
    in_specs = (
        P(("grp", "ex"), None, "proj"),
        P(("grp", "ex"), None, "proj"),
        P(("grp", "ex")),
        P(None, "proj"),
        P("proj", None),
        P("proj", None),
        P(),
        P(("grp", "ex"), "proj"),
    )
    out_specs = (P(("grp", "ex"), "proj"), P(("grp", "ex"), "proj"))
    return jax.shard_map(shards, mesh=mesh, in_specs=in_specs, out_specs=out_specs, check_vma=False)
```

```python
import functools
import math

import jax
import jax.numpy as jnp
from jax import lax
from jax.experimental import pallas as pl
from jax.experimental.pallas import tpu as pltpu
from jax.sharding import PartitionSpec as P

epsilon = 1e-06
LANES = 128
PLANES = 4
F32, BF16 = jnp.float32, jnp.bfloat16
NT = (((1,), (1,)), ((), ()))
HBM = pl.BlockSpec(memory_space=pltpu.HBM)
VMEM = pl.BlockSpec(memory_space=pltpu.VMEM)
PARAMS = pltpu.CompilerParams(vmem_limit_bytes=48 * 1024 * 1024)


def swap(x, axis, mask):
    size = lax.axis_size(axis)
    return lax.ppermute(x, axis, [(i, i ^ mask) for i in range(size)])


def dot(a, b, dims=(((1,), (0,)), ((), ()))):
    return lax.dot_general(a, b, dims, preferred_element_type=F32)


def open_kernel(out):
    out[...] = jnp.zeros_like(out)


def opening():
    return pl.pallas_call(
        open_kernel,
        out_shape=pltpu.VMEM((8, LANES), F32),
        out_specs=VMEM,
        compiler_params=pltpu.CompilerParams(vmem_limit_bytes=63400000),
        cost_estimate=pl.CostEstimate(flops=20_000_000_000, bytes_accessed=400_000_000, transcendentals=0),
        name="opening",
    )()


def rank_kernel(acts, cots, down, up, sketch, _, right):
    k2 = sketch.shape[1]
    folded = [dot(sketch[0], down[...]), dot(sketch[1], up[...], NT)]
    sums = []
    for p, keep in enumerate((acts, cots)):
        coarse = folded[p].astype(BF16).astype(F32)
        weights = jnp.concatenate([coarse, folded[p] - coarse], axis=0).astype(BF16)
        got = dot(weights, keep[...], NT)
        sums.append(got[:k2] + got[k2:])
    right[...] = jnp.concatenate(sums, axis=0).astype(right.dtype)


def rank_side(acts, cots, down, up, sketch, gate):
    rows = acts.shape[0]
    return pl.pallas_call(
        rank_kernel,
        out_shape=jax.ShapeDtypeStruct((2 * sketch.shape[1], rows), BF16),
        in_specs=[VMEM] * 5 + [pl.BlockSpec(memory_space=pl.ANY)],
        out_specs=VMEM,
        compiler_params=PARAMS,
        name="rank_side",
    )(acts, cots, down, up, sketch, gate)


def sums_kernel(n_proj, seq_len, k2, *refs):
    rights, (lengths, acts, cots, width, *outs, parted) = refs[:n_proj], refs[n_proj:]
    right = sum([r[...].astype(F32) for r in rights[1:]], rights[0][...].astype(F32))
    ex_dev, rows = lengths.shape[1], acts.shape[0]
    t = lax.broadcasted_iota(jnp.int32, (k2, rows), 1)
    wide = []
    for p, keep in enumerate((cots, acts)):
        own = right[p * k2 : (p + 1) * k2]
        own = own.astype(BF16).astype(F32)
        spread = [
            jnp.where((t >= e * seq_len) & (t < e * seq_len + lengths[:, e : e + 1]), own, 0.0) for e in range(ex_dev)
        ]
        wide.append(dot(jnp.concatenate(spread, axis=0).astype(BF16), keep[...]))
    both = [wide[p][e * k2 : (e + 1) * k2] for e in range(ex_dev) for p in range(2)]
    total = dot(jnp.concatenate(both, axis=0).astype(BF16), width[...])
    k_own = width.shape[1] // n_proj
    for s in range(n_proj):
        parted[s] = total[:, s * k_own : (s + 1) * k_own]
    me = lax.axis_index("proj")
    for m in range(n_proj):
        outs[m][...] = parted[me ^ m].astype(outs[m].dtype)


def token_sums(rights, lengths, acts, cots, width, seq_len, k2):
    n_proj = len(rights)
    ex_dev = lengths.shape[1]
    shape = (ex_dev * 2 * k2, width.shape[1] // n_proj)
    return pl.pallas_call(
        functools.partial(sums_kernel, n_proj, seq_len, k2),
        out_shape=[jax.ShapeDtypeStruct(shape, F32)] + [jax.ShapeDtypeStruct(shape, BF16)] * (n_proj - 1),
        in_specs=[VMEM] * n_proj + [VMEM] + [VMEM] * 3,
        out_specs=[VMEM] * n_proj,
        scratch_shapes=[pltpu.VMEM((n_proj,) + shape, F32)],
        compiler_params=PARAMS,
        name="token_sums",
        cost_estimate=pl.CostEstimate(flops=20000000000, bytes_accessed=400000000, transcendentals=0),
    )(*rights, lengths, acts, cots, width)


def dots_kernel(n_proj, r, *refs):
    pieces, lengths, blocks = refs[:n_proj], refs[n_proj], refs[n_proj + 1 : -4]
    train, note, turned, lined = refs[-4:]
    ex_dev = lengths.shape[1]
    k_own = pieces[0].shape[1]
    low = LANES // r
    high = k_own // low
    total = sum([piece[...].astype(F32) for piece in pieces[1:]], pieces[0][...].astype(F32))
    scaled = [total[e * r : (e + 1) * r] / lengths[:, e : e + 1].astype(F32) for e in range(ex_dev)]
    turned[:, : ex_dev * r] = jnp.concatenate(scaled, axis=0).T
    lane = lax.broadcasted_iota(jnp.int32, (high, LANES), 1)
    lines = [jnp.zeros((high, LANES), F32)] * ex_dev
    for lo in range(low):
        got = turned[pl.ds(lo, high, stride=low), :]
        for e in range(ex_dev):
            moved = got if lo == e else pltpu.roll(got, (lo - e) * r % LANES, 1)
            lines[e] = jnp.where((lane >= lo * r) & (lane < (lo + 1) * r), moved, lines[e])
    for e in range(ex_dev):
        lined[pl.ds(e, high, stride=ex_dev), :] = lines[e]
    squares = jnp.zeros((ex_dev, LANES), F32)
    for hi in range(high):
        line = lined[hi * ex_dev : (hi + 1) * ex_dev, :].astype(BF16)
        train[:, hi * LANES : (hi + 1) * LANES] = line
        squares += line.astype(F32) * line.astype(F32)
    own = train[...]
    note[...] = jnp.zeros_like(note)
    at, rows, group = 0, 0, []
    for block in blocks:
        for begin in range(0, block.shape[0], LANES):
            size = min(LANES, block.shape[0] - begin)
            group.append(block[begin : begin + size, :])
            rows += size
            if rows == LANES:
                values = jnp.concatenate(group, axis=0)
                note[:ex_dev, at : at + LANES] = dot(own, values, NT)
                square = jnp.zeros((LANES, LANES), F32)
                for c in range(0, values.shape[1], LANES):
                    piece = values[:, c : c + LANES].astype(F32)
                    square += piece * piece
                note[ex_dev : ex_dev + 1, at : at + LANES] = jnp.sum(square.T, axis=0, keepdims=True)
                at, rows, group = at + LANES, 0, []
    note[:ex_dev, at : at + LANES] = jnp.broadcast_to(jnp.sum(squares, axis=1, keepdims=True), (ex_dev, LANES))


def partial_dots(pieces, lengths, blocks, r):
    n_proj, ex_dev = len(pieces), lengths.shape[1]
    k_own = pieces[0].shape[1]
    n_val = sum(block.shape[0] for block in blocks)
    high = k_own * r // LANES
    return pl.pallas_call(
        functools.partial(dots_kernel, n_proj, r),
        out_shape=(
            pltpu.VMEM((ex_dev, k_own * r), BF16),
            jax.ShapeDtypeStruct((2 * ex_dev, n_val + LANES), F32),
        ),
        in_specs=[VMEM] * n_proj + [VMEM] + [VMEM] * len(blocks),
        out_specs=(VMEM, VMEM),
        scratch_shapes=[pltpu.VMEM((k_own, LANES), F32), pltpu.VMEM((high * ex_dev, LANES), F32)],
        compiler_params=PARAMS,
        name="partial_dots",
    )(*pieces, lengths, *blocks)


def scores_kernel(n_proj, ex_dev, scale, by_mask, *refs):
    notes, out = refs[:n_proj], refs[n_proj]
    total = sum([note[...] for note in notes[1:]], notes[0][...])
    n_val = total.shape[1] - LANES
    share = out.shape[1]
    train_sq = total[:ex_dev, n_val : n_val + 1]
    val_sq = total[ex_dev : ex_dev + 1, :n_val]
    every = scale * total[:ex_dev, :n_val] * lax.rsqrt(train_sq + epsilon) * lax.rsqrt(val_sq + epsilon)
    at = lax.axis_index("proj")
    if by_mask:
        at = at ^ lax.axis_index("ex")
    whole = jnp.concatenate([every, every], axis=0)
    out[...] = pltpu.roll(whole, (n_val - at * share) % n_val, 1)[:ex_dev, :share]


def final_scores(notes, ex_dev, share, scale, by_mask):
    return pl.pallas_call(
        functools.partial(scores_kernel, len(notes), ex_dev, scale, by_mask),
        out_shape=jax.ShapeDtypeStruct((ex_dev, share), F32),
        in_specs=[VMEM] * len(notes),
        out_specs=VMEM,
        compiler_params=PARAMS,
        name="final_scores",
    )(*notes)


def shards(
    inputs,
    cotangents,
    lengths,
    adapter_down_matrix,
    adapter_up_matrix,
    width_side_sketch,
    rank_side_sketch,
    heldout_gradient_rows,
):
    ex_dev, seq_len, model_cols = inputs.shape
    rows = ex_dev * seq_len
    k1, k2 = width_side_sketch.shape[1], rank_side_sketch.shape[2]
    n_proj, n_ex = lax.axis_size("proj"), lax.axis_size("ex")
    lengths = lengths.reshape(1, ex_dev)
    acts = inputs.reshape(rows, model_cols)
    cots = cotangents.reshape(rows, model_cols)

    by_mask = n_ex == n_proj == PLANES
    if by_mask:
        gate, held = lax.optimization_barrier((opening(), heldout_gradient_rows))
        blocks = [heldout_gradient_rows] * n_ex
        blocks[3] = swap(held, "ex", 3)
    else:
        gate = opening()
        blocks = [lax.all_gather(heldout_gradient_rows, "ex", axis=0, tiled=True)]

    right = rank_side(
        acts, cots, adapter_down_matrix, adapter_up_matrix, rank_side_sketch.transpose(0, 2, 1), gate
    )
    rights = [right] + [swap(right, "proj", m) for m in range(1, n_proj)]
    if by_mask:
        blocks[1] = swap(heldout_gradient_rows, "ex", 1)
        blocks[2] = swap(blocks[3], "ex", 1)
    pieces = token_sums(rights, lengths, acts, cots, width_side_sketch, seq_len, k2)
    pieces = [pieces[0]] + [swap(pieces[m], "proj", m) for m in range(n_proj - 1, 0, -1)]
    train_proj, note = partial_dots(pieces, lengths, blocks, 2 * k2)
    notes = [note] + [swap(note, "proj", m) for m in range(1, n_proj)]
    share = (note.shape[1] - LANES) // n_proj
    scores = final_scores(notes, ex_dev, share, math.sqrt(k1 * 2 * k2), by_mask)
    return (train_proj, scores)


def solution(mesh):
    in_specs = (
        P(("grp", "ex"), None, "proj"),
        P(("grp", "ex"), None, "proj"),
        P(("grp", "ex")),
        P(None, "proj"),
        P("proj", None),
        P("proj", None),
        P(),
        P(("grp", "ex"), "proj"),
    )
    out_specs = (P(("grp", "ex"), "proj"), P(("grp", "ex"), "proj"))
    return jax.shard_map(shards, mesh=mesh, in_specs=in_specs, out_specs=out_specs, check_vma=False)
```

```python
import functools
import math

import jax
import jax.numpy as jnp
from jax import lax
from jax.experimental import pallas as pl
from jax.experimental.pallas import tpu as pltpu
from jax.sharding import PartitionSpec as P

epsilon = 1e-06
LANES = 128
PLANES = 4
F32, BF16 = jnp.float32, jnp.bfloat16
NT = (((1,), (1,)), ((), ()))
HBM = pl.BlockSpec(memory_space=pltpu.HBM)
VMEM = pl.BlockSpec(memory_space=pltpu.VMEM)
PARAMS = pltpu.CompilerParams(vmem_limit_bytes=48 * 1024 * 1024)


def swap(x, axis, mask):
    size = lax.axis_size(axis)
    return lax.ppermute(x, axis, [(i, i ^ mask) for i in range(size)])


def dot(a, b, dims=(((1,), (0,)), ((), ()))):
    return lax.dot_general(a, b, dims, preferred_element_type=F32)


def open_kernel(out):
    out[...] = jnp.zeros_like(out)


def opening():
    return pl.pallas_call(
        open_kernel,
        out_shape=pltpu.VMEM((8, LANES), F32),
        out_specs=VMEM,
        compiler_params=pltpu.CompilerParams(vmem_limit_bytes=63400000),
        cost_estimate=pl.CostEstimate(flops=20_000_000_000, bytes_accessed=400_000_000, transcendentals=0),
        name="opening",
    )()


def rank_kernel(acts, cots, down, up, sketch, _, right):
    k2 = sketch.shape[1]
    folded = [dot(sketch[0], down[...]), dot(sketch[1], up[...], NT)]
    sums = []
    for p, keep in enumerate((acts, cots)):
        coarse = folded[p].astype(BF16).astype(F32)
        weights = jnp.concatenate([coarse, folded[p] - coarse], axis=0).astype(BF16)
        got = dot(weights, keep[...], NT)
        sums.append(got[:k2] + got[k2:])
    right[...] = jnp.concatenate(sums, axis=0).astype(right.dtype)


def rank_side(acts, cots, down, up, sketch, gate):
    rows = acts.shape[0]
    return pl.pallas_call(
        rank_kernel,
        out_shape=jax.ShapeDtypeStruct((2 * sketch.shape[1], rows), BF16),
        in_specs=[VMEM] * 5 + [pl.BlockSpec(memory_space=pl.ANY)],
        out_specs=VMEM,
        compiler_params=PARAMS,
        name="rank_side",
    )(acts, cots, down, up, sketch, gate)


def sums_kernel(n_proj, seq_len, k2, *refs):
    rights, (lengths, acts, cots, width, *outs, parted) = refs[:n_proj], refs[n_proj:]
    right = sum([r[...].astype(F32) for r in rights[1:]], rights[0][...].astype(F32))
    ex_dev, rows = lengths.shape[1], acts.shape[0]
    t = lax.broadcasted_iota(jnp.int32, (k2, rows), 1)
    wide = []
    for p, keep in enumerate((cots, acts)):
        own = right[p * k2 : (p + 1) * k2]
        own = own.astype(BF16).astype(F32)
        spread = [
            jnp.where((t >= e * seq_len) & (t < e * seq_len + lengths[:, e : e + 1]), own, 0.0) for e in range(ex_dev)
        ]
        wide.append(dot(jnp.concatenate(spread, axis=0).astype(BF16), keep[...]))
    both = [wide[p][e * k2 : (e + 1) * k2] for e in range(ex_dev) for p in range(2)]
    total = dot(jnp.concatenate(both, axis=0).astype(BF16), width[...])
    k_own = width.shape[1] // n_proj
    for s in range(n_proj):
        parted[s] = total[:, s * k_own : (s + 1) * k_own]
    me = lax.axis_index("proj")
    for m in range(n_proj):
        outs[m][...] = parted[me ^ m].astype(outs[m].dtype)


def token_sums(rights, lengths, acts, cots, width, seq_len, k2):
    n_proj = len(rights)
    ex_dev = lengths.shape[1]
    shape = (ex_dev * 2 * k2, width.shape[1] // n_proj)
    return pl.pallas_call(
        functools.partial(sums_kernel, n_proj, seq_len, k2),
        out_shape=[jax.ShapeDtypeStruct(shape, F32)] + [jax.ShapeDtypeStruct(shape, BF16)] * (n_proj - 1),
        in_specs=[VMEM] * n_proj + [VMEM] + [VMEM] * 3,
        out_specs=[VMEM] * n_proj,
        scratch_shapes=[pltpu.VMEM((n_proj,) + shape, F32)],
        compiler_params=PARAMS,
        name="token_sums",
        cost_estimate=pl.CostEstimate(flops=20000000000, bytes_accessed=400000000, transcendentals=0),
    )(*rights, lengths, acts, cots, width)


def dots_kernel(n_proj, r, *refs):
    pieces, lengths, blocks = refs[:n_proj], refs[n_proj], refs[n_proj + 1 : -4]
    train, note, turned, lined = refs[-4:]
    ex_dev = lengths.shape[1]
    k_own = pieces[0].shape[1]
    low = LANES // r
    high = k_own // low
    total = sum([piece[...].astype(F32) for piece in pieces[1:]], pieces[0][...].astype(F32))
    scaled = [total[e * r : (e + 1) * r] / lengths[:, e : e + 1].astype(F32) for e in range(ex_dev)]
    turned[:, : ex_dev * r] = jnp.concatenate(scaled, axis=0).T
    lane = lax.broadcasted_iota(jnp.int32, (high, LANES), 1)
    lines = [jnp.zeros((high, LANES), F32)] * ex_dev
    for lo in range(low):
        got = turned[pl.ds(lo, high, stride=low), :]
        for e in range(ex_dev):
            moved = got if lo == e else pltpu.roll(got, (lo - e) * r % LANES, 1)
            lines[e] = jnp.where((lane >= lo * r) & (lane < (lo + 1) * r), moved, lines[e])
    for e in range(ex_dev):
        lined[pl.ds(e, high, stride=ex_dev), :] = lines[e]
    squares, own = jnp.zeros((ex_dev, LANES), F32), []
    for hi in range(high):
        line = lined[hi * ex_dev : (hi + 1) * ex_dev, :].astype(BF16)
        train[:, hi * LANES : (hi + 1) * LANES] = line
        own.append(line)
        squares += line.astype(F32) * line.astype(F32)
    own = jnp.concatenate(own, axis=1)
    note[...] = jnp.zeros_like(note)
    at, rows, group = 0, 0, []
    for block in blocks:
        for begin in range(0, block.shape[0], LANES):
            size = min(LANES, block.shape[0] - begin)
            group.append(block[begin : begin + size, :])
            rows += size
            if rows == LANES:
                values = jnp.concatenate(group, axis=0)
                note[:ex_dev, at : at + LANES] = dot(own, values, NT)
                square = jnp.zeros((LANES, LANES), F32)
                for c in range(0, values.shape[1], LANES):
                    piece = values[:, c : c + LANES].astype(F32)
                    square += piece * piece
                note[ex_dev : ex_dev + 1, at : at + LANES] = jnp.sum(square.T, axis=0, keepdims=True)
                at, rows, group = at + LANES, 0, []
    total_sq = jnp.sum(squares, axis=1, keepdims=True)
    spot = lax.broadcasted_iota(jnp.int32, (ex_dev, LANES), 1) == lax.broadcasted_iota(jnp.int32, (ex_dev, LANES), 0)
    note[ex_dev + 1 : ex_dev + 2, :LANES] = jnp.sum(jnp.where(spot, total_sq, 0.0), axis=0, keepdims=True)


def partial_dots(pieces, lengths, blocks, r):
    n_proj, ex_dev = len(pieces), lengths.shape[1]
    k_own = pieces[0].shape[1]
    n_val = sum(block.shape[0] for block in blocks)
    high = k_own * r // LANES
    return pl.pallas_call(
        functools.partial(dots_kernel, n_proj, r),
        out_shape=(
            pltpu.VMEM((ex_dev, k_own * r), BF16),
            jax.ShapeDtypeStruct((2 * ex_dev, n_val), F32),
        ),
        in_specs=[VMEM] * n_proj + [VMEM] + [VMEM] * len(blocks),
        out_specs=(VMEM, VMEM),
        scratch_shapes=[pltpu.VMEM((k_own, LANES), F32), pltpu.VMEM((high * ex_dev, LANES), F32)],
        compiler_params=PARAMS,
        name="partial_dots",
    )(*pieces, lengths, *blocks)


def scores_kernel(n_proj, ex_dev, scale, by_mask, *refs):
    notes, out = refs[:n_proj], refs[n_proj]
    total = sum([note[...] for note in notes[1:]], notes[0][...])
    n_val = total.shape[1]
    share = out.shape[1]
    spot = lax.broadcasted_iota(jnp.int32, (ex_dev, LANES), 1) == lax.broadcasted_iota(jnp.int32, (ex_dev, LANES), 0)
    squares = jnp.broadcast_to(total[ex_dev + 1 : ex_dev + 2, :LANES], (ex_dev, LANES))
    train_sq = jnp.sum(jnp.where(spot, squares, 0.0), axis=1, keepdims=True)
    val_sq = total[ex_dev : ex_dev + 1, :n_val]
    every = scale * total[:ex_dev, :n_val] * lax.rsqrt(train_sq + epsilon) * lax.rsqrt(val_sq + epsilon)
    at = lax.axis_index("proj")
    if by_mask:
        at = at ^ lax.axis_index("ex")
    whole = jnp.concatenate([every, every], axis=0)
    out[...] = pltpu.roll(whole, (n_val - at * share) % n_val, 1)[:ex_dev, :share]


def final_scores(notes, ex_dev, share, scale, by_mask):
    return pl.pallas_call(
        functools.partial(scores_kernel, len(notes), ex_dev, scale, by_mask),
        out_shape=jax.ShapeDtypeStruct((ex_dev, share), F32),
        in_specs=[VMEM] * len(notes),
        out_specs=VMEM,
        compiler_params=PARAMS,
        name="final_scores",
    )(*notes)


def shards(
    inputs,
    cotangents,
    lengths,
    adapter_down_matrix,
    adapter_up_matrix,
    width_side_sketch,
    rank_side_sketch,
    heldout_gradient_rows,
):
    ex_dev, seq_len, model_cols = inputs.shape
    rows = ex_dev * seq_len
    k1, k2 = width_side_sketch.shape[1], rank_side_sketch.shape[2]
    n_proj, n_ex = lax.axis_size("proj"), lax.axis_size("ex")
    lengths = lengths.reshape(1, ex_dev)
    acts = inputs.reshape(rows, model_cols)
    cots = cotangents.reshape(rows, model_cols)

    by_mask = n_ex == n_proj == PLANES
    if by_mask:
        gate, held = lax.optimization_barrier((opening(), heldout_gradient_rows))
        blocks = [heldout_gradient_rows] * n_ex
        blocks[3] = swap(held, "ex", 3)
    else:
        gate = opening()
        blocks = [lax.all_gather(heldout_gradient_rows, "ex", axis=0, tiled=True)]

    right = rank_side(
        acts, cots, adapter_down_matrix, adapter_up_matrix, rank_side_sketch.transpose(0, 2, 1), gate
    )
    rights = [right] + [swap(right, "proj", m) for m in range(1, n_proj)]
    if by_mask:
        blocks[1] = swap(heldout_gradient_rows, "ex", 1)
        blocks[2] = swap(blocks[3], "ex", 1)
    pieces = token_sums(rights, lengths, acts, cots, width_side_sketch, seq_len, k2)
    pieces = [pieces[0]] + [swap(pieces[m], "proj", m) for m in range(n_proj - 1, 0, -1)]
    train_proj, note = partial_dots(pieces, lengths, blocks, 2 * k2)
    notes = [note] + [swap(note, "proj", m) for m in range(1, n_proj)]
    share = note.shape[1] // n_proj
    scores = final_scores(notes, ex_dev, share, math.sqrt(k1 * 2 * k2), by_mask)
    return (train_proj, scores)


def solution(mesh):
    in_specs = (
        P(("grp", "ex"), None, "proj"),
        P(("grp", "ex"), None, "proj"),
        P(("grp", "ex")),
        P(None, "proj"),
        P("proj", None),
        P("proj", None),
        P(),
        P(("grp", "ex"), "proj"),
    )
    out_specs = (P(("grp", "ex"), "proj"), P(("grp", "ex"), "proj"))
    return jax.shard_map(shards, mesh=mesh, in_specs=in_specs, out_specs=out_specs, check_vma=False)
```
